32 devices in a mesh: grp: 2 (over x), ctg: 16 (over z, y, core).
Axes of the slice: x: 2, y: 2, z: 4, core: 2. Of those that a mesh axis runs over, the one named last changes fastest.
Arguments:
- flow_tiles: bfloat16 [128, 256, 3072], P('ctg'), may hold values from -0.109375 to 0.109375
- tile_pattern: int32 [128, 2, 24], P('ctg'), may hold values 0 or 1
- monitored: int32 [128, 256], P('ctg'), may hold values from 0 to 16383
- ratings: float32 [16384], replicated, may hold values from 0.3 to 3
- base_flow: float32 [64, 128, 256], P('grp', 'ctg'), parts along dimension 0, may hold values from -6 to 6
- unit_cost: float32 [64, 3072], P(('grp', 'ctg')), parts along dimension 0, may hold values from -6 to 6
- unit_floor: float32 [3072], replicated, may hold values from 0 to 0.5
- unit_span: float32 [3072], replicated, may hold values from 0.5 to 2
- ramp_limit: float32 [3072], replicated, may hold values from 0.05 to 0.5
- ramp_mask: int32 [3072], replicated, may hold values 0 or 1
- demand: float32 [64], P(('grp', 'ctg')), parts along dimension 0, may hold values from 1228.8 to 2457.6
- start_output: float32 [64, 3072], P(('grp', 'ctg')), parts along dimension 0, may hold values from 0 to 1.5
- start_flow_dual: float32 [64, 128, 256], P('grp', 'ctg'), parts along dimension 0, may hold values from -2 to 2
- start_ramp_dual: float32 [64, 3072], P(('grp', 'ctg')), parts along dimension 0, may hold values from -3 to 3
Outputs:
- output_levels: float32 [64, 3072], P(('grp', 'ctg')), parts along dimension 0
- flow_dual: float32 [64, 128, 256], P('grp', 'ctg'), parts along dimension 0
- ramp_dual: float32 [64, 3072], P(('grp', 'ctg')), parts along dimension 0
- balance_price: float32 [64], P(('grp', 'ctg')), parts along dimension 0
The draws below stay inside these ranges and needn't reach their ends.
There are 2 independent parts, one for each index of `grp`. The reference program is written for one: setup_inputs(seed, part) draws one part's arguments, and reference() takes and returns one part's arrays. A program takes and returns all parts, laid end to end along the dimension named above; an argument that names none is the same for every part. Nothing has to cross between parts.
All inputs are finite; a program needn't handle non-finite values. No bound on the sum of `tile_pattern` on one device may be relied on, other than what follows from the above.
Results may differ from the reference program's by a relative error of at most 0.0045.
Values may be sent and summed in bfloat16 or wider, within the bound.
No kernel may reach another device: no remote copies, remote signals or barrier semaphores. Data moves between devices by JAX's collectives and lax.ppermute only.
A program may use at most 128 MiB of HBM per device.

```python
import math
import jax
import jax.numpy as jnp
from jax import lax

UNITS = 3072
MON = 256
LINES = 16384
ITERS = 4
CTGS = 128
HOURS = 32


def draw_base_flow(key, part):
    severity = 0.5 + jnp.arange(CTGS, dtype=jnp.float32) / CTGS
    values = jnp.clip(jax.random.normal(key, (HOURS, CTGS, MON), jnp.float32), -4.0, 4.0)
    return values * severity[None, :, None]


def set_ends(result, own_key, smallest, high):
    longest = result.shape.index(max(result.shape))
    spots = []
    for shift in (0, 1):
        where = [jax.random.randint(jax.random.fold_in(own_key, axis), (), 0, length) for axis, length in enumerate(result.shape)]
        where[longest] = (where[longest] + shift) % result.shape[longest]
        spots.append(tuple(where))
    return result.at[spots[0]].set(smallest).at[spots[1]].set(high)


def shard_levels(key, dims, shards, smallest, high):
    gain = 1.0
    for dim, shards_of in shards:
        draws = jax.random.uniform(jax.random.fold_in(jax.random.fold_in(key, 6), dim), (shards_of,), jnp.float32, smallest / len(shards), high / len(shards))
        gain = gain * jnp.repeat(jnp.exp(draws), dims[dim] // shards_of).reshape((-1,) + (1,) * (len(dims) - 1 - dim))
    return gain


def centred(key, dims, width, limit, pieces=(), held_as=jnp.bfloat16):
    level = shard_levels(key, dims, pieces, -0.22, 0.18) if pieces else 1.0
    drawn = jax.random.normal(key, dims, jnp.float32) * width * level
    return jnp.minimum(jnp.maximum(drawn, -limit), limit).astype(held_as)


def setup_inputs(seed: int = 0, part: int = 0) -> dict:
    splits = jax.random.split(jax.random.key(seed), 15)
    part_splits = jax.random.split(jax.random.fold_in(splits[14], part), 15)
    flow_tiles = centred(splits[0], (CTGS, MON, UNITS), UNITS ** -0.5, 0.109375, ((0, 16),))
    tile_pattern = set_ends((jax.random.randint(splits[1], (CTGS, MON // 128, UNITS // 128), 0, 2) < 1).astype(jnp.int32), jax.random.fold_in(splits[1], 1), 0, 1)
    monitored = set_ends(jax.random.randint(splits[2], (CTGS, MON), 0, LINES), jax.random.fold_in(splits[2], 1), 0, LINES - 1).astype(jnp.int32)
    ratings = jnp.clip(jnp.exp(jax.random.uniform(splits[3], (LINES,), jnp.float32, math.log(0.3), math.log(3.0))), 0.3, 3.0)
    base_flow = draw_base_flow(jax.random.fold_in(jax.random.fold_in(splits[14], part), 71), part)
    unit_cost = centred(part_splits[5], (HOURS, UNITS), 1.0, 6.0, ((0, 16),), jnp.float32)
    unit_floor = jnp.clip(jax.random.uniform(splits[6], (UNITS,), jnp.float32, 0.0, 0.5), 0.0, 0.5)
    unit_span = jnp.clip(jnp.exp(jax.random.uniform(splits[7], (UNITS,), jnp.float32, math.log(0.5), math.log(2.0))), 0.5, 2.0)
    ramp_limit = jnp.clip(jnp.exp(jax.random.uniform(splits[8], (UNITS,), jnp.float32, math.log(0.05), math.log(0.5))), 0.05, 0.5)
    ramp_mask = set_ends((jax.random.randint(splits[9], (UNITS,), 0, 4) < 3).astype(jnp.int32), jax.random.fold_in(splits[9], 1), 0, 1)
    demand = jnp.clip(1228.8 + 1228.8 * jax.random.uniform(part_splits[10], (HOURS,), jnp.float32) ** shard_levels(part_splits[10], (HOURS,), ((0, 16),), -0.2, 0.2), 1228.8, 2457.6)
    start_output = jnp.clip(1.5 * jax.random.uniform(part_splits[11], (HOURS, UNITS), jnp.float32) ** shard_levels(part_splits[11], (HOURS, UNITS), ((0, 16),), -0.2, 0.2), 0.0, 1.5)
    start_flow_dual = centred(part_splits[12], (HOURS, CTGS, MON), 0.3, 2.0, ((1, 16),), jnp.float32)
    start_ramp_dual = centred(part_splits[13], (HOURS, UNITS), 0.5, 3.0, ((0, 16),), jnp.float32)
    return {"flow_tiles": flow_tiles, "tile_pattern": tile_pattern, "monitored": monitored, "ratings": ratings, "base_flow": base_flow, "unit_cost": unit_cost, "unit_floor": unit_floor, "unit_span": unit_span, "ramp_limit": ramp_limit, "ramp_mask": ramp_mask, "demand": demand, "start_output": start_output, "start_flow_dual": start_flow_dual, "start_ramp_dual": start_ramp_dual}


def mask_tiles(flow_tiles, tile_pattern):
    ctg_count, line_count, unit_count = flow_tiles.shape
    blocks = flow_tiles.reshape(ctg_count, line_count // 128, 128, unit_count // 128, 128)
    gates = tile_pattern.astype(jnp.bfloat16)[:, :, None, :, None]
    return (blocks * gates).reshape(ctg_count, line_count, unit_count)

def reference(flow_tiles, tile_pattern, monitored, ratings, base_flow, unit_cost, unit_floor, unit_span, ramp_limit, ramp_mask, demand, start_output, start_flow_dual, start_ramp_dual):
    masked = mask_tiles(flow_tiles, tile_pattern).astype(jnp.float32)
    flow_limit = ratings[monitored]
    flow_lower = base_flow - flow_limit[None]
    flow_upper = base_flow + flow_limit[None]
    step_size = 0.5 / (2.0 + math.sqrt(CTGS * MON / UNITS))
    balance = 1.0 / math.sqrt(UNITS)
    ceiling = unit_floor + unit_span
    ramp_on = ramp_mask.astype(jnp.float32)
    weight = jnp.float32(1.0)
    levels = start_output
    flow_dual = start_flow_dual
    ramp_dual = start_ramp_dual
    balance_price = jnp.zeros((HOURS,), jnp.float32)
    zero_row = jnp.zeros((1, UNITS), jnp.float32)
    for iteration in range(ITERS):
        primal_step = step_size / weight
        dual_step = step_size * weight
        dual_half = lax.optimization_barrier(flow_dual.astype(jnp.bfloat16)).astype(jnp.float32)
        pulled = jnp.einsum('tkm,kmu->tu', dual_half, masked, precision=lax.Precision.HIGHEST)
        before = jnp.concatenate([zero_row, ramp_dual[:-1]], axis=0)
        gradient = unit_cost + pulled + ramp_on * (before - ramp_dual) + balance * balance_price[:, None]
        moved = jnp.clip(levels - primal_step * gradient, unit_floor, ceiling)
        extended = 2.0 * moved - levels
        extended_half = lax.optimization_barrier(extended.astype(jnp.bfloat16)).astype(jnp.float32)
        flows = jnp.einsum('kmu,tu->tkm', masked, extended_half, precision=lax.Precision.HIGHEST)
        trial = flow_dual + dual_step * flows
        dual_new = trial - dual_step * jnp.clip(trial / dual_step, flow_lower, flow_upper)
        change = ramp_on * jnp.concatenate([extended[1:] - extended[:-1], zero_row], axis=0)
        ramp_trial = ramp_dual + dual_step * change
        ramp_new = ramp_trial - dual_step * jnp.clip(ramp_trial / dual_step, -ramp_limit, ramp_limit)
        balance_row = balance * (lax.optimization_barrier(jnp.sum(extended, axis=1)) - demand)
        price_new = balance_price + dual_step * balance_row
        if iteration < ITERS - 1:
            primal_sq = jnp.sum((moved - levels) ** 2)
            dual_sq = jnp.sum((dual_new - flow_dual) ** 2) + jnp.sum((ramp_new - ramp_dual) ** 2) + jnp.sum((price_new - balance_price) ** 2)
            weight = jnp.sqrt(weight) * ((dual_sq + 1e-06) / (primal_sq + 1e-06)) ** 0.25
        levels = moved
        flow_dual = dual_new
        ramp_dual = ramp_new
        balance_price = price_new
    return (levels, flow_dual, ramp_dual, balance_price)
```

```python
import functools
import math

import jax
import jax.numpy as jnp
from jax import lax
from jax.experimental import pallas as pl
from jax.experimental.pallas import tpu as pltpu
from jax.sharding import PartitionSpec as P

ITERS = 4
LANES = 128
WIDE = 256
MIB = 2**20
HALF = jnp.bfloat16
FULL = jnp.float32

VMEM = pl.BlockSpec(memory_space=pltpu.VMEM)
SMEM = pl.BlockSpec(memory_space=pltpu.SMEM)
HBM = pl.BlockSpec(memory_space=pltpu.HBM)


def total(x):
    return jnp.sum(jnp.sum(x, axis=1, keepdims=True), axis=0, keepdims=True)


def add_rows(values, first, rows):
    row = lax.broadcasted_iota(jnp.int32, values.shape, 0)
    for j, extra in enumerate(rows):
        values = values + jnp.where(row == first + j, extra, 0.0)
    return values


def hour_terms(cost, ramp, on, price_terms):
    hours = len(cost)
    rows = []
    for j in range(hours + 1):
        if j == hours:
            rows.append(on * ramp[j - 1])
            continue
        row = cost[j] + on * ((ramp[j - 1] if j else 0.0) - ramp[j])
        if price_terms is not None:
            row = row + price_terms[j]
        rows.append(row)
    return rows


def scalar_block(value, place, shape):
    row = lax.broadcasted_iota(jnp.int32, shape, 0)
    lane = lax.broadcasted_iota(jnp.int32, shape, 1)
    block = jnp.zeros(shape, FULL)
    left = value
    for j in range(3):
        part = left.astype(HALF).astype(FULL)
        left = left - part
        block = block + jnp.where((row == j) & (lane == place), part, 0.0)
    return block.astype(HALF)


def own_first(place, s, width):
    core = place % 2
    return pl.multiple_of((core if s == 0 else 1 - core) * width, LANES)


def start_kernel(
    place_ref,
    gate_ref,
    tiles_ref,
    dual_ref,
    base_ref,
    monitored_ref,
    ratings_ref,
    floor_ref,
    span_ref,
    limit_ref,
    on_ref,
    cost_ref,
    ramp_ref,
    masked_ref,
    send_ref,
    keep_ref,
    dual_out,
    base_out,
    rating_out,
    unit_out,
    cost_out,
    ramp_out,
    acc_ref,
    sems,
):
    ctgs, lines, units = masked_ref.shape
    width = units // 2
    half_tiles = width // LANES
    hours = cost_ref.shape[0]
    place = place_ref[0]

    def copy(k, s):
        return pltpu.make_async_copy(
            tiles_ref.at[k, :, pl.ds(own_first(place, s, width), width)],
            masked_ref.at[k, :, pl.ds(s * width, width)],
            sems.at[k, s],
        )

    for k in range(ctgs):
        for s in range(2):
            copy(k, s).start()

    table = ratings_ref[...].T
    hi = table.astype(HALF)
    left = table - hi.astype(FULL)
    mid = left.astype(HALF)
    lo = (left - mid.astype(FULL)).astype(HALF)
    groups = table.shape[1]
    for k in range(ctgs):
        cols = pl.ds(k * lines, lines)
        dual_out[:, cols] = dual_ref[:, k, :]
        base_out[:, cols] = base_ref[:, k, :]
        index = monitored_ref[k : k + 1, :]
        group = lax.broadcasted_iota(jnp.int32, (groups, lines), 0)
        chosen = (group == index // LANES).astype(FULL).astype(HALF)
        picked = (
            jnp.dot(hi, chosen, preferred_element_type=FULL)
            + jnp.dot(mid, chosen, preferred_element_type=FULL)
            + jnp.dot(lo, chosen, preferred_element_type=FULL)
        )
        lane = lax.broadcasted_iota(jnp.int32, (LANES, lines), 0)
        rating_out[:, cols] = jnp.sum(jnp.where(lane == index % LANES, picked, 0.0), axis=0, keepdims=True)
    for s in range(2):
        cols, own = pl.ds(s * width, width), pl.ds(own_first(place, s, width), width)
        floor = floor_ref[:, own]
        unit_out[0:1, cols] = floor
        unit_out[1:2, cols] = floor + span_ref[:, own]
        unit_out[2:3, cols] = limit_ref[:, own]
        unit_out[3:4, cols] = on_ref[:, own].astype(FULL)
        cost_out[:, cols] = cost_ref[:, own]
        ramp_out[:, cols] = ramp_ref[:, own]

    for k in range(ctgs):
        lhs = dual_out[:, pl.ds(k * lines, lines)].astype(HALF)
        for s in range(2):
            copy(k, s).wait()
            gate_at = (place % 2 if s == 0 else 1 - place % 2) * half_tiles
            for j in range(0, half_tiles, 2):
                at = s * width + j * LANES
                block = []
                for m in range(lines // LANES):
                    line = []
                    for i in range(2):
                        gate = gate_ref[k, m, gate_at + j + i]
                        part = masked_ref[k, pl.ds(m * LANES, LANES), pl.ds(at + i * LANES, LANES)]
                        line.append(jnp.where(gate > 0, part, jnp.zeros((), HALF)))
                    block.append(jnp.concatenate(line, axis=1))
                block = jnp.concatenate(block, axis=0)
                cols = pl.ds(at, WIDE)
                masked_ref[k, :, cols] = block
                part = jnp.dot(lhs, block, preferred_element_type=FULL)
                acc_ref[:, cols] = part if k == 0 else acc_ref[:, cols] + part

    for s, out_ref in ((1, send_ref), (0, keep_ref)):
        cols = pl.ds(s * width, width)
        on = unit_out[3:4, cols]
        cost = [cost_out[j : j + 1, cols] for j in range(hours)]
        ramp = [ramp_out[j : j + 1, cols] for j in range(hours)]
        rows = hour_terms(cost, ramp, on, None)
        out_ref[:, :width] = add_rows(acc_ref[:, cols], place * hours, rows).astype(HALF)
        out_ref[:, width:] = jnp.zeros((out_ref.shape[0], LANES), HALF)


def step_kernel(step_size, balance, first, last, *refs):
    refs = list(refs)
    place_ref, masked_ref, own_ref, other_ref = refs[:4]
    del refs[:4]
    level_refs = [refs.pop(0) for _ in range(2 if first else 1)]
    stat_ref = None if first else refs.pop(0)
    dual_ref, base_ref, rating_ref, unit_ref, cost_ref, demand_ref, ramp_ref = refs[:7]
    del refs[:7]
    price_ref = None if first else refs.pop(0)
    level_out, dual_out, ramp_out, price_out = refs[:4]
    del refs[:4]
    if not last:
        send_ref, keep_ref, stat_out, half_dual = refs[:4]
        del refs[:4]
    extended_ref, half_ref = refs[:2]
    moved_ref = refs[2] if last else level_out

    ctgs, lines, units = masked_ref.shape
    width = units // 2
    all_hours = own_ref.shape[0]
    hours = cost_ref.shape[0]
    place = place_ref[0]
    first_hour = place * hours

    if first:
        weight = jnp.full((1, 1), 1.0, FULL)
    else:
        dual_sq = total(own_ref[:, width:].astype(FULL))
        primal_sq = stat_ref[1:2, 0:1]
        weight = jnp.sqrt(stat_ref[0:1, 0:1]) * jnp.sqrt(jnp.sqrt((dual_sq + 1e-06) / (primal_sq + 1e-06)))
    primal_step = step_size / weight
    dual_step = step_size * weight

    if first:
        for d in range(all_hours // hours):
            for s in range(2):
                block = place ^ d ^ s
                for j in range(hours):
                    level_out[pl.ds(d * hours + j, 1), pl.ds(s * width, width)] = level_refs[s][
                        pl.ds(block * hours + j, 1), :
                    ]
        level_refs = [level_out]
    primal_acc = jnp.zeros((all_hours, WIDE), FULL)
    for at in range(0, units, WIDE):
        cols = pl.ds(at, WIDE)
        s, inner = at // width, pl.ds(at % width, WIDE)
        gradient = (own_ref, other_ref)[s][:, inner].astype(FULL)
        levels = level_refs[0][:, cols]
        moved = jnp.clip(levels - primal_step * gradient, unit_ref[0:1, cols], unit_ref[1:2, cols])
        extended = 2.0 * moved - levels
        moved_ref[:, cols] = moved
        extended_ref[:, cols] = extended
        half_ref[:, cols] = extended.astype(HALF)
        if not last:
            primal_acc = primal_acc + (moved - levels) ** 2

    flow_acc = jnp.zeros((all_hours, lines), FULL)
    for k in range(ctgs):
        cols = pl.ds(k * lines, lines)
        flows = lax.dot_general(
            half_ref[...], masked_ref[k], (((1,), (1,)), ((), ())), preferred_element_type=FULL
        )
        old = dual_ref[:, cols]
        trial = old + dual_step * flows
        base, rating = base_ref[:, cols], rating_ref[:, cols]
        new = trial - jnp.clip(trial, dual_step * (base - rating), dual_step * (base + rating))
        if last:
            dual_out[:, k, :] = new
        else:
            dual_out[:, cols] = new
            half_dual[:, cols] = new.astype(HALF)
            flow_acc = flow_acc + (new - old) ** 2

    ramp_limit, ramp_on = unit_ref[2:3, :], unit_ref[3:4, :]
    moved_sq = total(flow_acc)
    rows, ramp_rows, price_rows = [], [], []
    for j in range(hours + 1):
        rows.append(extended_ref[pl.ds(jnp.minimum(first_hour + j, all_hours - 1), 1), :])
    for j in range(hours):
        old = ramp_ref[j : j + 1, :]
        trial = old + dual_step * (ramp_on * (rows[j + 1] - rows[j]))
        reach = dual_step * ramp_limit
        new = trial - jnp.clip(trial, -reach, reach)
        old_price = jnp.zeros((1, 1), FULL) if first else price_ref[j : j + 1, :]
        supply = jnp.sum(rows[j], axis=1, keepdims=True)
        new_price = old_price + dual_step * (balance * (supply - demand_ref[0:1, j : j + 1]))
        if last:
            price_out[j] = new_price[0, 0]
        else:
            price_out[j : j + 1, :] = new_price
        moved_sq = moved_sq + total((new - old) ** 2) + (new_price - old_price) ** 2
        ramp_rows.append(new)
        price_rows.append(new_price)
        if last:
            for s in range(2):
                own = pl.ds(own_first(place, s, width), width)
                level_out[j : j + 1, own] = moved_ref[pl.ds(first_hour + j, 1), pl.ds(s * width, width)]
                ramp_out[j : j + 1, own] = new[:, s * width : (s + 1) * width]
        else:
            ramp_out[j : j + 1, :] = new
    if last:
        return

    primal_sq = total(primal_acc)
    row = lax.broadcasted_iota(jnp.int32, stat_out.shape, 0)
    stat_out[...] = jnp.where(row == 0, weight, primal_sq)
    block = scalar_block(moved_sq, place, (all_hours, LANES))
    price_terms = [balance * price for price in price_rows]
    whole = masked_ref.reshape(ctgs * lines, units)
    for s, out_ref in ((1, send_ref), (0, keep_ref)):
        out_ref[:, width:] = block
        for at in range(0, width, WIDE):
            cols = pl.ds(s * width + at, WIDE)
            pulled = jnp.dot(half_dual[...], whole[:, cols], preferred_element_type=FULL)
            here = slice(s * width + at, s * width + at + WIDE)
            terms = hour_terms(
                [cost_ref[j : j + 1, cols] for j in range(hours)],
                [ramp[:, here] for ramp in ramp_rows],
                ramp_on[:, here],
                price_terms,
            )
            out_ref[:, pl.ds(at, WIDE)] = add_rows(pulled, first_hour, terms).astype(HALF)


def exchange(x, mask):
    devices = lax.axis_size("ctg")
    return lax.ppermute(x, "ctg", [(i, i ^ mask) for i in range(devices)])


def far_masks():
    devices = lax.axis_size("ctg")
    assert devices & (devices - 1) == 0 and 2 <= devices <= LANES
    return [1 << b for b in range(1, devices.bit_length() - 1)]


def sum_over_devices(send, keep):
    own = keep + exchange(send, 1)
    for mask in far_masks():
        own = own + exchange(own, mask)
    return own, exchange(own, 1)


def split_kernel(place_ref, x_ref, own_ref, other_ref):
    width = x_ref.shape[1] // 2
    for s, out_ref in ((0, own_ref), (1, other_ref)):
        out_ref[...] = x_ref[:, pl.ds(own_first(place_ref[0], s, width), width)]


def join_kernel(first_ref, second_ref, out_ref):
    rows = first_ref.shape[0]
    out_ref[:rows, :] = first_ref[...]
    out_ref[rows:, :] = second_ref[...]


def join(first, second):
    return pl.pallas_call(
        join_kernel,
        out_shape=jax.ShapeDtypeStruct((2 * first.shape[0], first.shape[1]), first.dtype),
        in_specs=[VMEM, VMEM],
        out_specs=VMEM,
        compiler_params=params(12),
        name="join",
    )(first, second)


def gather_levels(here, levels):
    half = jax.ShapeDtypeStruct((levels.shape[0], levels.shape[1] // 2), FULL)
    own, other = pl.pallas_call(
        split_kernel,
        out_shape=(half, half),
        in_specs=[SMEM, VMEM],
        out_specs=(VMEM, VMEM),
        compiler_params=params(12),
        name="split",
    )(here, levels)
    own = join(own, exchange(other, 1))
    for mask in far_masks():
        own = join(own, exchange(own, mask))
    return own, exchange(own, 1)


def params(limit):
    return pltpu.CompilerParams(vmem_limit_bytes=limit * MIB)


def body(
    flow_tiles,
    tile_pattern,
    monitored,
    ratings,
    base_flow,
    unit_cost,
    unit_floor,
    unit_span,
    ramp_limit,
    ramp_mask,
    demand,
    start_output,
    start_flow_dual,
    start_ramp_dual,
):
    ctgs, lines, units = flow_tiles.shape
    all_hours, hours = start_flow_dual.shape[0], start_output.shape[0]
    devices = lax.axis_size("ctg")
    place = lax.axis_index("ctg")
    here = place.astype(jnp.int32).reshape(1)
    width = units // 2
    step_size = 0.5 / (2.0 + math.sqrt(ctgs * devices * lines / units))
    balance = 1.0 / math.sqrt(units)
    spread = -ratings.shape[0] % (8 * LANES)
    table = jnp.pad(ratings, (0, spread)).reshape(-1, LANES)
    row = lambda x: x.reshape(1, units)
    f32 = lambda *shape: jax.ShapeDtypeStruct(shape, FULL)
    near = lambda *shape: pltpu.VMEM(shape, FULL)
    message = pltpu.VMEM((all_hours, width + LANES), HALF)

    masked, send, keep, dual, base, rating, unit, cost, ramp = pl.pallas_call(
        start_kernel,
        out_shape=(
            pltpu.VMEM(flow_tiles.shape, HALF),
            message,
            message,
            near(all_hours, ctgs * lines),
            near(all_hours, ctgs * lines),
            near(1, ctgs * lines),
            near(4, units),
            near(hours, units),
            near(hours, units),
        ),
        in_specs=[SMEM, SMEM, HBM] + [VMEM] * 10,
        out_specs=(VMEM,) * 9,
        scratch_shapes=[pltpu.VMEM((all_hours, units), FULL), pltpu.SemaphoreType.DMA((ctgs, 2))],
        compiler_params=params(44),
        name="start",
    )(
        here,
        tile_pattern,
        flow_tiles,
        start_flow_dual,
        base_flow,
        monitored,
        table,
        row(unit_floor),
        row(unit_span),
        row(ramp_limit),
        row(ramp_mask),
        unit_cost,
        start_ramp_dual,
    )
    masked = pltpu.with_memory_space_constraint(masked, pltpu.VMEM)
    levels = gather_levels(here, start_output)
    demands = demand.reshape(1, hours)
    stat = ()
    for iteration in range(ITERS):
        first, last = iteration == 0, iteration == ITERS - 1
        own, other = sum_over_devices(send, keep)
        out_shape = [near(all_hours, units), near(all_hours, ctgs * lines), near(hours, units), near(hours, 1)]
        scratch = [pltpu.VMEM((all_hours, units), FULL), pltpu.VMEM((all_hours, units), HALF)]
        if last:
            out_shape = [f32(hours, units), f32(all_hours, ctgs, lines), f32(hours, units), f32(hours)]
            scratch.append(pltpu.VMEM((all_hours, units), FULL))
        else:
            out_shape += [message, message, near(8, LANES)]
            scratch.insert(0, pltpu.VMEM((all_hours, ctgs * lines), HALF))
        operands = [here, masked, own, other, *levels, *stat]
        operands += [dual, base, rating, unit, cost, demands, ramp] + ([] if first else [price])
        outs = pl.pallas_call(
            functools.partial(step_kernel, step_size, balance, first, last),
            out_shape=tuple(out_shape),
            in_specs=[SMEM] + [VMEM] * (len(operands) - 1),
            out_specs=tuple(SMEM if last and j == 3 else VMEM for j in range(len(out_shape))),
            scratch_shapes=scratch,
            compiler_params=params(12),
            name="step",
        )(*operands)
        levels, dual, ramp, price = (outs[0],), outs[1], outs[2], outs[3]
        if not last:
            send, keep, stat = outs[4], outs[5], (outs[6],)
    return levels[0], dual, ramp, price


def solution(mesh):
    return jax.shard_map(
        body,
        mesh=mesh,
        in_specs=(
            P("ctg", None, None),
            P("ctg", None, None),
            P("ctg", None),
            P(),
            P("grp", "ctg", None),
            P(("grp", "ctg"), None),
            P(),
            P(),
            P(),
            P(),
            P(("grp", "ctg")),
            P(("grp", "ctg"), None),
            P("grp", "ctg", None),
            P(("grp", "ctg"), None),
        ),
        out_specs=(
            P(("grp", "ctg"), None),
            P("grp", "ctg", None),
            P(("grp", "ctg"), None),
            P(("grp", "ctg")),
        ),
        check_vma=False,
    )
```

```python
import functools
import math

import jax
import jax.numpy as jnp
from jax import lax
from jax.experimental import pallas as pl
from jax.experimental.pallas import tpu as pltpu
from jax.sharding import PartitionSpec as P

ITERS = 4
LANES = 128
WIDE = 256
MIB = 2**20
HALF = jnp.bfloat16
FULL = jnp.float32

PIECES = 4

VMEM = pl.BlockSpec(memory_space=pltpu.VMEM)
SMEM = pl.BlockSpec(memory_space=pltpu.SMEM)
HBM = pl.BlockSpec(memory_space=pltpu.HBM)


def near(*shape, dtype=FULL):
    return pltpu.VMEM(shape, dtype)


def far(x):
    return pltpu.with_memory_space_constraint(x, pltpu.HBM)


def call(kernel, name, us, operands, out_shape, scratch=(), smem=(), smem_out=(), limit=12):
    return pl.pallas_call(
        kernel,
        out_shape=tuple(out_shape),
        in_specs=[SMEM if j in smem else VMEM for j in range(len(operands))],
        out_specs=tuple(SMEM if j in smem_out else VMEM for j in range(len(out_shape))),
        scratch_shapes=list(scratch),
        compiler_params=pltpu.CompilerParams(vmem_limit_bytes=limit * MIB),
        cost_estimate=pl.CostEstimate(flops=0, bytes_accessed=int(us * 3.69e6), transcendentals=0),
        name=name,
    )(*operands)


def total(x):
    return jnp.sum(jnp.sum(x, axis=1, keepdims=True), axis=0, keepdims=True)


def piece_at(piece, units):
    return (piece % 2) * (units // 2) + (piece // 2) * (units // 4)


def own_first(place, s, width):
    core = place % 2
    return pl.multiple_of((core if s == 0 else 1 - core) * width, LANES)


def add_rows(values, first, rows):
    row = lax.broadcasted_iota(jnp.int32, values.shape, 0)
    for j, extra in enumerate(rows):
        values = values + jnp.where(row == first + j, extra, 0.0)
    return values


def hour_terms(cost, ramp, on, price_terms):
    hours = len(cost)
    rows = []
    for j in range(hours + 1):
        if j == hours:
            rows.append(on * ramp[j - 1])
            continue
        row = cost[j] + on * ((ramp[j - 1] if j else 0.0) - ramp[j])
        if price_terms is not None:
            row = row + price_terms[j]
        rows.append(row)
    return rows


def scalar_block(value, place, shape):
    row = lax.broadcasted_iota(jnp.int32, shape, 0)
    lane = lax.broadcasted_iota(jnp.int32, shape, 1)
    block = jnp.zeros(shape, FULL)
    left = value
    for j in range(3):
        part = left.astype(HALF).astype(FULL)
        left = left - part
        block = block + jnp.where((row == j) & (lane == place), part, 0.0)
    return block.astype(HALF)


def start_kernel(
    place_ref,
    gate_hbm,
    tiles_ref,
    dual_ref,
    base_ref,
    monitored_ref,
    ratings_ref,
    floor_ref,
    span_ref,
    limit_ref,
    on_ref,
    cost_ref,
    ramp_ref,
    level_ref,
    masked_ref,
    send_a,
    keep_a,
    send_b,
    keep_b,
    dual_out,
    base_out,
    rating_out,
    unit_out,
    cost_out,
    ramp_out,
    gate_ref,
    acc_ref,
    sems,
    gate_sem,
):
    ctgs, lines, units = masked_ref.shape
    width, quarter = units // 2, units // 4
    half_tiles = width // LANES
    all_hours, hours = dual_ref.shape[0], cost_ref.shape[0]
    place = place_ref[0]

    def copy(k, s):
        return pltpu.make_async_copy(
            tiles_ref.at[k, :, pl.ds(own_first(place, s, width), width)],
            masked_ref.at[k, :, pl.ds(s * width, width)],
            sems.at[k, s],
        )

    gates = pltpu.make_async_copy(gate_hbm, gate_ref, gate_sem)
    gates.start()
    for k in range(ctgs):
        for s in range(2):
            copy(k, s).start()

    table = ratings_ref[...].T
    hi = table.astype(HALF)
    left = table - hi.astype(FULL)
    mid = left.astype(HALF)
    lo = (left - mid.astype(FULL)).astype(HALF)
    groups = table.shape[1]
    for k in range(ctgs):
        cols = pl.ds(k * lines, lines)
        dual_out[:, cols] = dual_ref[:, k, :]
        base_out[:, cols] = base_ref[:, k, :]
        index = monitored_ref[k : k + 1, :]
        group = lax.broadcasted_iota(jnp.int32, (groups, lines), 0)
        chosen = (group == index // LANES).astype(FULL).astype(HALF)
        picked = (
            jnp.dot(hi, chosen, preferred_element_type=FULL)
            + jnp.dot(mid, chosen, preferred_element_type=FULL)
            + jnp.dot(lo, chosen, preferred_element_type=FULL)
        )
        lane = lax.broadcasted_iota(jnp.int32, (LANES, lines), 0)
        rating_out[:, cols] = jnp.sum(jnp.where(lane == index % LANES, picked, 0.0), axis=0, keepdims=True)
    for s in range(2):
        cols, own = pl.ds(s * width, width), pl.ds(own_first(place, s, width), width)
        floor = floor_ref[:, own]
        unit_out[0:1, cols] = floor
        unit_out[1:2, cols] = floor + span_ref[:, own]
        unit_out[2:3, cols] = limit_ref[:, own]
        unit_out[3:4, cols] = on_ref[:, own].astype(FULL)
        cost_out[:, cols] = cost_ref[:, own]
        ramp_out[:, cols] = ramp_ref[:, own]

    gates.wait()
    for k in range(ctgs):
        lhs = dual_out[:, pl.ds(k * lines, lines)].astype(HALF)
        for s in range(2):
            copy(k, s).wait()
            gate_at = (place % 2 if s == 0 else 1 - place % 2) * half_tiles
            for j in range(0, half_tiles, 2):
                at = s * width + j * LANES
                block = []
                for m in range(lines // LANES):
                    line = []
                    for i in range(2):
                        gate = gate_ref[k, m, gate_at + j + i]
                        part = masked_ref[k, pl.ds(m * LANES, LANES), pl.ds(at + i * LANES, LANES)]
                        line.append(jnp.where(gate > 0, part, jnp.zeros((), HALF)))
                    block.append(jnp.concatenate(line, axis=1))
                block = jnp.concatenate(block, axis=0)
                cols = pl.ds(at, WIDE)
                masked_ref[k, :, cols] = block
                part = jnp.dot(lhs, block, preferred_element_type=FULL)
                acc_ref[:, cols] = part if k == 0 else acc_ref[:, cols] + part

    for piece, out_ref in enumerate((keep_a, send_a, keep_b, send_b)):
        cols = pl.ds(piece_at(piece, units), quarter)
        rows = hour_terms(
            [cost_out[j : j + 1, cols] for j in range(hours)],
            [ramp_out[j : j + 1, cols] for j in range(hours)],
            unit_out[3:4, cols],
            None,
        )
        values = add_rows(acc_ref[:, cols], place * hours, rows)
        own = pl.multiple_of(own_first(place, piece % 2, width) + (piece // 2) * quarter, LANES)
        level = level_ref[:, pl.ds(own, quarter)]
        high = level.astype(HALF).astype(FULL)
        message = jnp.concatenate([values, high, level - high], axis=0)
        rest = out_ref.shape[1] - quarter
        if rest:
            message = jnp.concatenate([message, jnp.zeros((out_ref.shape[0], rest), FULL)], axis=1)
        out_ref[...] = message.astype(HALF)


def turn_kernel(first_ctg, masked_ref, before_ref, out_ref):
    ctgs, units, lines = out_ref.shape
    for k in range(ctgs):
        for at in range(0, units, WIDE):
            out_ref[k, pl.ds(at, WIDE), :] = masked_ref[first_ctg + k, :, pl.ds(at, WIDE)].T


def starting_levels(piece, devices, place, message_ref, all_hours, quarter):
    hours = all_hours // devices
    levels = message_ref[all_hours:, :quarter]
    shape = (all_hours, levels.shape[0])
    hour = lax.broadcasted_iota(jnp.int32, shape, 0)
    row = lax.broadcasted_iota(jnp.int32, shape, 1)
    apart = place ^ (hour // hours) ^ (piece % 2)
    block = jnp.zeros(shape, jnp.int32)
    for bit, mask in enumerate([1] + mask_order(devices, piece // 2)):
        block = block + ((apart // mask) % 2) * 2**bit
    chosen = (row // (2 * hours) == block) & (row % hours == hour % hours)
    return jnp.dot(chosen.astype(FULL).astype(HALF), levels, preferred_element_type=FULL)


def primal_piece(piece, step_size, stat_ref, message_ref, levels, unit_ref, moved_ref):
    all_hours, quarter = levels.shape
    cols = pl.ds(piece_at(piece, unit_ref.shape[1]), quarter)
    primal_step = step_size / stat_ref[0:1, 0:1]
    gradient = message_ref[:all_hours, :quarter].astype(FULL)
    moved = jnp.clip(levels - primal_step * gradient, unit_ref[0:1, cols], unit_ref[1:2, cols])
    moved_ref[...] = moved
    return (2.0 * moved - levels).astype(HALF)


def piece_flows(piece, half, turned_refs, k):
    turned_ref = turned_refs[k // turned_refs[0].shape[0]]
    rows = pl.ds(piece_at(piece, turned_ref.shape[1]), half.shape[1])
    return jnp.dot(half, turned_ref[k % turned_refs[0].shape[0], rows, :], preferred_element_type=FULL)


def flow_kernel(step_size, piece, devices, turns, first, *refs):
    refs = list(refs)
    turned_refs = [refs.pop(0) for _ in range(turns)]
    place_ref = refs.pop(0)
    message_ref, unit_ref = refs[:2]
    del refs[:2]
    level_ref = None if first else refs.pop(0)
    stat_ref = None if first and piece == 0 else refs.pop(0)
    flow_ref = refs.pop(0) if piece else None
    moved_ref, flow_out = refs[:2]
    del refs[:2]
    all_hours, quarter = moved_ref.shape
    if first:
        level_out = refs.pop(0)
        levels = starting_levels(piece, devices, place_ref[0], message_ref, all_hours, quarter)
        level_out[...] = levels
    else:
        levels = level_ref[...]
    if piece == 0:
        stat_out = refs.pop(0)
        if first:
            stat_out[...] = jnp.full(stat_out.shape, 1.0, FULL)
        else:
            dual_sq = total(message_ref[:all_hours, quarter:].astype(FULL))
            primal_sq = stat_ref[1:2, 0:1]
            ratio = (dual_sq + 1e-06) / (primal_sq + 1e-06)
            weight = jnp.sqrt(stat_ref[0:1, 0:1]) * jnp.sqrt(jnp.sqrt(ratio))
            stat_out[...] = jnp.broadcast_to(weight, stat_out.shape)
        stat_ref = stat_out
    half = primal_piece(piece, step_size, stat_ref, message_ref, levels, unit_ref, moved_ref)
    lines = turned_refs[0].shape[2]
    for k in range(turns * turned_refs[0].shape[0]):
        at = pl.ds(k * lines, lines)
        part = piece_flows(piece, half, turned_refs, k)
        flow_out[:, at] = part if flow_ref is None else flow_ref[:, at] + part


def dual_kernel(step_size, balance, devices, turns, first, last, *refs):
    refs = list(refs)
    turned_refs = [refs.pop(0) for _ in range(turns)]
    place_ref, masked_ref, message_ref = refs[:3]
    del refs[:3]
    level_refs = [refs.pop(0) for _ in range(3 if first else 4)]
    moved_refs = [refs.pop(0) for _ in range(3)]
    stat_ref, flow_ref, dual_ref, base_ref, rating_ref, unit_ref, cost_ref, demand_ref, ramp_ref = refs[:9]
    del refs[:9]
    price_ref = None if first else refs.pop(0)
    if first:
        level_refs.append(refs.pop())
    if last:
        level_out, dual_out, ramp_out, price_out, last_moved = refs
    else:
        last_moved, dual_out, ramp_out, price_out, stat_out, send_ref, keep_ref, half_dual, term_out = refs
    moved_refs = moved_refs + [last_moved]

    ctgs, lines, units = masked_ref.shape
    width, quarter = units // 2, units // 4
    all_hours, hours = level_refs[0].shape[0], cost_ref.shape[0]
    place = place_ref[0]
    first_hour = place * hours
    weight = stat_ref[0:1, 0:1]
    dual_step = step_size * weight

    if first:
        level_refs[3][...] = starting_levels(3, devices, place, message_ref, all_hours, quarter)
    half = primal_piece(3, step_size, stat_ref, message_ref, level_refs[3][...], unit_ref, last_moved)
    flow_acc = jnp.zeros((all_hours, lines), FULL)
    for k in range(ctgs):
        at = pl.ds(k * lines, lines)
        flows = flow_ref[:, at] + piece_flows(3, half, turned_refs, k)
        old = dual_ref[:, at]
        trial = old + dual_step * flows
        base, rating = base_ref[:, at], rating_ref[:, at]
        new = trial - jnp.clip(trial, dual_step * (base - rating), dual_step * (base + rating))
        if last:
            dual_out[:, k, :] = new
        else:
            dual_out[:, at] = new
            half_dual[:, at] = new.astype(HALF)
            flow_acc = flow_acc + (new - old) ** 2

    places = [pl.ds(piece_at(piece, units), quarter) for piece in range(PIECES)]
    moved_sq = None if last else total(flow_acc)
    supply = [jnp.zeros((1, 1), FULL) for _ in range(hours)]
    ramps = [[] for _ in range(hours)]
    for piece in range(PIECES):
        at = places[piece]
        ramp_limit, ramp_on = unit_ref[2:3, at], unit_ref[3:4, at]
        rows = []
        for j in range(hours + 1):
            spot = pl.ds(jnp.minimum(first_hour + j, all_hours - 1), 1)
            rows.append(2.0 * moved_refs[piece][spot, :] - level_refs[piece][spot, :])
        for j in range(hours):
            old = ramp_ref[j : j + 1, at]
            trial = old + dual_step * (ramp_on * (rows[j + 1] - rows[j]))
            reach = dual_step * ramp_limit
            new = trial - jnp.clip(trial, -reach, reach)
            supply[j] = supply[j] + jnp.sum(rows[j], axis=1, keepdims=True)
            ramps[j].append(new)
            if last:
                own = pl.multiple_of(own_first(place, piece % 2, width) + (piece // 2) * quarter, LANES)
                level_out[j : j + 1, pl.ds(own, quarter)] = moved_refs[piece][pl.ds(first_hour + j, 1), :]
                ramp_out[j : j + 1, pl.ds(own, quarter)] = new
            else:
                ramp_out[j : j + 1, at] = new
                moved_sq = moved_sq + total((new - old) ** 2)
    prices = []
    for j in range(hours):
        old = jnp.zeros((1, 1), FULL) if first else price_ref[j : j + 1, :]
        new = old + dual_step * (balance * (supply[j] - demand_ref[0:1, j : j + 1]))
        prices.append(balance * new)
        if last:
            price_out[j] = new[0, 0]
        else:
            price_out[j : j + 1, :] = new
            moved_sq = moved_sq + (new - old) ** 2
    if last:
        return

    primal_acc = jnp.zeros((all_hours, quarter), FULL)
    for piece in range(PIECES):
        primal_acc = primal_acc + (moved_refs[piece][...] - level_refs[piece][...]) ** 2
    row = lax.broadcasted_iota(jnp.int32, stat_out.shape, 0)
    stat_out[...] = jnp.where(row == 0, weight, total(primal_acc))
    for piece in range(PIECES):
        at = places[piece]
        terms = hour_terms(
            [cost_ref[j : j + 1, at] for j in range(hours)],
            [ramps[j][piece] for j in range(hours)],
            unit_ref[3:4, at],
            prices,
        )
        for j, term in enumerate(terms):
            term_out[j : j + 1, at] = term
    block = scalar_block(moved_sq, place, (all_hours, LANES))
    pull_pieces(0, hours, first_hour, masked_ref, half_dual, term_out, send_ref, keep_ref)
    for out_ref in (send_ref, keep_ref):
        out_ref[:, quarter:] = block


def pull_pieces(q, hours, first_hour, masked_ref, half_dual, term_ref, send_ref, keep_ref):
    ctgs, lines, units = masked_ref.shape
    whole = masked_ref.reshape(ctgs * lines, units)
    for piece, out_ref in ((2 * q + 1, send_ref), (2 * q, keep_ref)):
        for at in range(0, units // 4, WIDE):
            cols = pl.ds(piece_at(piece, units) + at, WIDE)
            pulled = jnp.dot(half_dual[...], whole[:, cols], preferred_element_type=FULL)
            terms = [term_ref[j : j + 1, cols] for j in range(hours + 1)]
            out_ref[:, pl.ds(at, WIDE)] = add_rows(pulled, first_hour, terms).astype(HALF)


def pull_kernel(hours, place_ref, masked_ref, half_dual, term_ref, send_ref, keep_ref):
    pull_pieces(1, hours, place_ref[0] * hours, masked_ref, half_dual, term_ref, send_ref, keep_ref)


def add_kernel(own_ref, received_ref, before_ref, out_ref):
    out_ref[...] = (own_ref[...].astype(FULL) + received_ref[...].astype(FULL)).astype(HALF)


def add_after(own, received, before):
    return call(add_kernel, "add", 0.1, [own, received, before], [near(*own.shape, dtype=HALF)])[0]


def join_kernel(all_hours, own_ref, received_ref, *refs):
    out_ref, scratch_ref = refs[-2:]
    extra = own_ref.shape[0] - all_hours
    own, received = own_ref[...].astype(FULL), received_ref[...].astype(FULL)
    scratch_ref[:all_hours, :] = own[:all_hours] + received[:all_hours]
    scratch_ref[all_hours : all_hours + extra, :] = own[all_hours:]
    scratch_ref[all_hours + extra :, :] = received[all_hours:]
    out_ref[...] = scratch_ref[...].astype(HALF)


def join(all_hours, own, received, *before):
    shape = (2 * own.shape[0] - all_hours, own.shape[1])
    kernel = functools.partial(join_kernel, all_hours)
    return call(kernel, "join", 0.2, [own, received, *before], [near(*shape, dtype=HALF)], [near(*shape)])[0]


def exchange(x, mask):
    devices = lax.axis_size("ctg")
    return lax.ppermute(x, "ctg", [(i, i ^ mask) for i in range(devices)])


def mask_order(devices, q):
    masks = [1 << b for b in range(1, devices.bit_length() - 1)]
    return masks if q == 0 else masks[-1:] + masks[:-1]


def body(
    flow_tiles,
    tile_pattern,
    monitored,
    ratings,
    base_flow,
    unit_cost,
    unit_floor,
    unit_span,
    ramp_limit,
    ramp_mask,
    demand,
    start_output,
    start_flow_dual,
    start_ramp_dual,
):
    ctgs, lines, units = flow_tiles.shape
    all_hours, hours = start_flow_dual.shape[0], start_output.shape[0]
    devices = lax.axis_size("ctg")
    here = lax.axis_index("ctg").astype(jnp.int32).reshape(1)
    quarter = units // 4
    assert devices & (devices - 1) == 0 and 2 <= devices <= LANES and quarter % WIDE == 0
    step_size = 0.5 / (2.0 + math.sqrt(ctgs * devices * lines / units))
    balance = 1.0 / math.sqrt(units)
    spread = -ratings.shape[0] % (8 * LANES)
    table = jnp.pad(ratings, (0, spread)).reshape(-1, LANES)
    row = lambda x: x.reshape(1, units)
    start_rows = all_hours + 2 * hours
    start_a, start_b = near(start_rows, quarter + LANES, dtype=HALF), near(start_rows, quarter, dtype=HALF)
    message_a, message_b = near(all_hours, quarter + LANES, dtype=HALF), near(all_hours, quarter, dtype=HALF)

    operands = [flow_tiles, start_flow_dual, base_flow, monitored, table, row(unit_floor), row(unit_span)]
    operands += [row(ramp_limit), row(ramp_mask), unit_cost, start_ramp_dual, start_output]
    masked, send_a, keep_a, send_b, keep_b, dual, base, rating, unit, cost, ramp = pl.pallas_call(
        start_kernel,
        out_shape=(
            near(ctgs, lines, units, dtype=HALF),
            start_a,
            start_a,
            start_b,
            start_b,
            near(all_hours, ctgs * lines),
            near(all_hours, ctgs * lines),
            near(1, ctgs * lines),
            near(4, units),
            near(hours, units),
            near(hours, units),
        ),
        in_specs=[SMEM, HBM, HBM] + [VMEM] * 11,
        out_specs=(VMEM,) * 11,
        scratch_shapes=[
            pltpu.SMEM(tile_pattern.shape, jnp.int32),
            near(all_hours, units),
            pltpu.SemaphoreType.DMA((ctgs, 2)),
            pltpu.SemaphoreType.DMA,
        ],
        compiler_params=pltpu.CompilerParams(vmem_limit_bytes=44 * MIB),
        name="start",
    )(here, far(tile_pattern), *[far(x) for x in operands])
    masked = pltpu.with_memory_space_constraint(masked, pltpu.VMEM)
    demands = demand.reshape(1, hours)
    price, stat, levels, turned = None, None, None, []
    for iteration in range(ITERS):
        first, last = iteration == 0, iteration == ITERS - 1
        merge = functools.partial(join, all_hours) if first else jnp.add
        owns = [merge(keep_a, exchange(send_a, 1)), merge(keep_b, exchange(send_b, 1))]
        orders = [mask_order(devices, q) for q in range(2)]
        steps = len(orders[0])
        for step in range(steps):
            before = []
            if first:
                for turn in range(ctgs * step // steps, ctgs * (step + 1) // steps):
                    before += call(
                        functools.partial(turn_kernel, turn),
                        "turn",
                        0.45,
                        [masked, owns[0]],
                        [near(1, units, lines, dtype=HALF)],
                    )
                turned += before
            owns[0] = merge(owns[0], exchange(owns[0], orders[0][step]), *before)
            if first or step < steps - 1:
                owns[1] = merge(owns[1], exchange(owns[1], orders[1][step]))
        messages = [owns[0], exchange(owns[0], 1)]
        moved, flows = [], None
        levels = [] if first else levels
        for piece in range(3):
            if piece == 2:
                if not first:
                    owns[1] = add_after(owns[1], exchange(owns[1], orders[1][-1]), after)
                messages += [owns[1], exchange(owns[1], 1)]
            operands = [*turned, here, messages[piece], unit]
            operands += [] if first else [levels[piece]]
            operands += [] if first and piece == 0 else [stat]
            operands += [flows] if piece else []
            out_shape = [near(all_hours, quarter), near(all_hours, ctgs * lines)]
            out_shape += [near(all_hours, quarter)] if first else []
            out_shape += [] if piece else [near(8, LANES)]
            kernel = functools.partial(flow_kernel, step_size, piece, devices, len(turned), first)
            outs = call(kernel, "flow", 0.7, operands, out_shape, smem=(len(turned),))
            moved.append(outs[0])
            flows = outs[1]
            if first:
                levels.append(outs[2])
            if piece == 0:
                stat = after = outs[-1]
        operands = [*turned, here, masked, messages[3], *levels, *moved, stat, flows, dual, base, rating, unit, cost]
        operands += [demands, ramp] if first else [demands, ramp, price]
        kernel = functools.partial(dual_kernel, step_size, balance, devices, len(turned), first, last)
        smem = (len(turned),)
        if last:
            f32 = lambda *shape: jax.ShapeDtypeStruct(shape, FULL)
            out_shape = [f32(hours, units), f32(all_hours, ctgs, lines), f32(hours, units), f32(hours)]
            return call(kernel, "dual", 1.2, operands, out_shape, [near(all_hours, quarter)], smem, (3,))
        out_shape = [near(all_hours, quarter), near(all_hours, ctgs * lines), near(hours, units), near(hours, 1)]
        out_shape += [near(8, LANES), message_a, message_a, near(all_hours, ctgs * lines, dtype=HALF), near(8, units)]
        scratch = [near(all_hours, quarter)] if first else []
        outs = call(kernel, "dual", 2.1, operands, out_shape, scratch, smem)
        levels = (*moved, outs[0])
        dual, ramp, price, stat, send_a, keep_a, half_dual, terms = outs[1:]
        operands = [here, masked, half_dual, terms]
        send_b, keep_b = call(
            functools.partial(pull_kernel, hours), "pull", 1.2, operands, [message_b, message_b], smem=(0,)
        )


def solution(mesh):
    return jax.shard_map(
        body,
        mesh=mesh,
        in_specs=(
            P("ctg", None, None),
            P("ctg", None, None),
            P("ctg", None),
            P(),
            P("grp", "ctg", None),
            P(("grp", "ctg"), None),
            P(),
            P(),
            P(),
            P(),
            P(("grp", "ctg")),
            P(("grp", "ctg"), None),
            P("grp", "ctg", None),
            P(("grp", "ctg"), None),
        ),
        out_specs=(
            P(("grp", "ctg"), None),
            P("grp", "ctg", None),
            P(("grp", "ctg"), None),
            P(("grp", "ctg")),
        ),
        check_vma=False,
    )
```

```python
import functools
import math

import jax
import jax.numpy as jnp
from jax import lax
from jax.experimental import pallas as pl
from jax.experimental.pallas import tpu as pltpu
from jax.sharding import PartitionSpec as P

ITERS = 4
LANES = 128
WIDE = 256
MIB = 2**20
HALF = jnp.bfloat16
FULL = jnp.float32

PIECES = 4
TURNS = (2, 3, 3)
ORDERS = ((0, 0), (2, 0), (0, 0), (2, 0))

VMEM = pl.BlockSpec(memory_space=pltpu.VMEM)
SMEM = pl.BlockSpec(memory_space=pltpu.SMEM)
HBM = pl.BlockSpec(memory_space=pltpu.HBM)


def near(*shape, dtype=FULL):
    return pltpu.VMEM(shape, dtype)


def far(x):
    return pltpu.with_memory_space_constraint(x, pltpu.HBM)


def call(kernel, name, us, operands, out_shape, scratch=(), smem=(), smem_out=(), limit=12):
    return pl.pallas_call(
        kernel,
        out_shape=tuple(out_shape),
        in_specs=[SMEM if j in smem else VMEM for j in range(len(operands))],
        out_specs=tuple(SMEM if j in smem_out else VMEM for j in range(len(out_shape))),
        scratch_shapes=list(scratch),
        compiler_params=pltpu.CompilerParams(vmem_limit_bytes=limit * MIB),
        cost_estimate=pl.CostEstimate(flops=0, bytes_accessed=int(us * 3.69e6), transcendentals=0),
        name=name,
    )(*operands)


def total(x):
    return jnp.sum(jnp.sum(x, axis=1, keepdims=True), axis=0, keepdims=True)


def piece_at(piece, units):
    return (piece % 2) * (units // 2) + (piece // 2) * (units // 4)


def parity(index):
    odd = index % 2
    for bit in range(1, LANES.bit_length() - 1):
        odd = odd ^ ((index // 2**bit) % 2)
    return odd


def own_first(place, s, width):
    side = parity(place)
    return pl.multiple_of((side if s == 0 else 1 - side) * width, LANES)


def add_rows(values, first, rows):
    row = lax.broadcasted_iota(jnp.int32, values.shape, 0)
    for j, extra in enumerate(rows):
        values = values + jnp.where(row == first + j, extra, 0.0)
    return values


def hour_terms(cost, ramp, on, price_terms):
    hours = len(cost)
    rows = []
    for j in range(hours + 1):
        if j == hours:
            rows.append(on * ramp[j - 1])
            continue
        row = cost[j] + on * ((ramp[j - 1] if j else 0.0) - ramp[j])
        if price_terms is not None:
            row = row + price_terms[j]
        rows.append(row)
    return rows


def scalar_block(value, place, shape):
    row = lax.broadcasted_iota(jnp.int32, shape, 0)
    lane = lax.broadcasted_iota(jnp.int32, shape, 1)
    block = jnp.zeros(shape, FULL)
    left = value
    for j in range(3):
        part = left.astype(HALF).astype(FULL)
        left = left - part
        block = block + jnp.where((row == j) & (lane == place), part, 0.0)
    return block.astype(HALF)


def start_kernel(
    place_ref,
    gate_hbm,
    tiles_ref,
    dual_ref,
    on_ref,
    cost_ref,
    ramp_ref,
    level_ref,
    masked_ref,
    send_ref,
    keep_ref,
    gate_ref,
    acc_ref,
    sems,
    gate_sem,
):
    ctgs, lines, units = masked_ref.shape
    width, quarter = units // 2, units // 4
    half_tiles = width // LANES
    all_hours, hours = dual_ref.shape[0], cost_ref.shape[0]
    place = place_ref[0]

    def copy(k, s):
        return pltpu.make_async_copy(
            tiles_ref.at[k, :, pl.ds(own_first(place, s, width), width)],
            masked_ref.at[k, :, pl.ds(s * width, width)],
            sems.at[k, s],
        )

    gates = pltpu.make_async_copy(gate_hbm, gate_ref, gate_sem)
    gates.start()
    for k in range(ctgs):
        for s in range(2):
            copy(k, s).start()

    gates.wait()
    for k in range(ctgs):
        lhs = dual_ref[:, k, :].astype(HALF)
        for s in range(2):
            copy(k, s).wait()
            gate_at = own_first(place, s, width) // LANES
            for j in range(0, half_tiles, 2):
                at = s * width + j * LANES
                block = []
                for m in range(lines // LANES):
                    line = []
                    for i in range(2):
                        gate = gate_ref[k, m, gate_at + j + i]
                        part = masked_ref[k, pl.ds(m * LANES, LANES), pl.ds(at + i * LANES, LANES)]
                        line.append(jnp.where(gate > 0, part, jnp.zeros((), HALF)))
                    block.append(jnp.concatenate(line, axis=1))
                block = jnp.concatenate(block, axis=0)
                cols = pl.ds(at, WIDE)
                masked_ref[k, :, cols] = block
                part = jnp.dot(lhs, block, preferred_element_type=FULL)
                acc_ref[:, cols] = part if k == 0 else acc_ref[:, cols] + part

    for s, out_ref in enumerate((keep_ref, send_ref)):
        message = []
        for piece in (s, 2 + s):
            cols = pl.ds(piece_at(piece, units), quarter)
            own = pl.ds(pl.multiple_of(own_first(place, s, width) + (piece // 2) * quarter, LANES), quarter)
            rows = hour_terms(
                [cost_ref[j : j + 1, own] for j in range(hours)],
                [ramp_ref[j : j + 1, own] for j in range(hours)],
                on_ref[:, own].astype(FULL),
                None,
            )
            values = add_rows(acc_ref[:, cols], place * hours, rows)
            level = level_ref[:, own]
            high = level.astype(HALF).astype(FULL)
            message.append(jnp.concatenate([values, high, level - high], axis=0))
        out_ref[...] = jnp.concatenate(message, axis=1).astype(HALF)


def prepare_kernel(
    place_ref,
    before_ref,
    dual_ref,
    base_ref,
    monitored_ref,
    ratings_ref,
    floor_ref,
    span_ref,
    limit_ref,
    on_ref,
    cost_ref,
    ramp_ref,
    dual_out,
    base_out,
    rating_out,
    unit_out,
    cost_out,
    ramp_out,
):
    ctgs, lines = monitored_ref.shape
    width = floor_ref.shape[1] // 2
    place = place_ref[0]
    table = ratings_ref[...].T
    hi = table.astype(HALF)
    left = table - hi.astype(FULL)
    mid = left.astype(HALF)
    lo = (left - mid.astype(FULL)).astype(HALF)
    groups = table.shape[1]
    for k in range(ctgs):
        cols = pl.ds(k * lines, lines)
        dual_out[:, cols] = dual_ref[:, k, :]
        base_out[:, cols] = base_ref[:, k, :]
        index = monitored_ref[k : k + 1, :]
        group = lax.broadcasted_iota(jnp.int32, (groups, lines), 0)
        chosen = (group == index // LANES).astype(FULL).astype(HALF)
        picked = (
            jnp.dot(hi, chosen, preferred_element_type=FULL)
            + jnp.dot(mid, chosen, preferred_element_type=FULL)
            + jnp.dot(lo, chosen, preferred_element_type=FULL)
        )
        lane = lax.broadcasted_iota(jnp.int32, (LANES, lines), 0)
        rating_out[:, cols] = jnp.sum(jnp.where(lane == index % LANES, picked, 0.0), axis=0, keepdims=True)
    for s in range(2):
        cols, own = pl.ds(s * width, width), pl.ds(own_first(place, s, width), width)
        floor = floor_ref[:, own]
        unit_out[0:1, cols] = floor
        unit_out[1:2, cols] = floor + span_ref[:, own]
        unit_out[2:3, cols] = limit_ref[:, own]
        unit_out[3:4, cols] = on_ref[:, own].astype(FULL)
        cost_out[:, cols] = cost_ref[:, own]
        ramp_out[:, cols] = ramp_ref[:, own]


def turn_kernel(first_ctg, masked_ref, before_ref, out_ref):
    ctgs, units, lines = out_ref.shape
    for k in range(ctgs):
        for at in range(0, units, WIDE):
            out_ref[k, pl.ds(at, WIDE), :] = masked_ref[first_ctg + k, :, pl.ds(at, WIDE)].T


def starting_levels(piece, devices, place, message_ref, all_hours, quarter):
    hours = all_hours // devices
    levels = message_ref[all_hours:, :quarter]
    shape = (all_hours, levels.shape[0])
    hour = lax.broadcasted_iota(jnp.int32, shape, 0)
    row = lax.broadcasted_iota(jnp.int32, shape, 1)
    apart = place ^ (hour // hours) ^ (piece % 2)
    block = parity(apart)
    for bit, mask in enumerate(mask_order(devices, piece // 2, True)):
        block = block + ((apart // mask) % 2) * 2 ** (bit + 1)
    chosen = (row // (2 * hours) == block) & (row % hours == hour % hours)
    return jnp.dot(chosen.astype(FULL).astype(HALF), levels, preferred_element_type=FULL)


def primal_piece(piece, step_size, stat_ref, message_ref, levels, unit_ref, moved_ref):
    all_hours, quarter = levels.shape
    cols = pl.ds(piece_at(piece, unit_ref.shape[1]), quarter)
    primal_step = step_size / stat_ref[0:1, 0:1]
    gradient = message_ref[:all_hours, :quarter].astype(FULL)
    moved = jnp.clip(levels - primal_step * gradient, unit_ref[0:1, cols], unit_ref[1:2, cols])
    moved_ref[...] = moved
    return (2.0 * moved - levels).astype(HALF)


def piece_flows(piece, half, turned_refs, k):
    turned_ref = turned_refs[k // turned_refs[0].shape[0]]
    rows = pl.ds(piece_at(piece, turned_ref.shape[1]), half.shape[1])
    return jnp.dot(half, turned_ref[k % turned_refs[0].shape[0], rows, :], preferred_element_type=FULL)


def flow_kernel(step_size, piece, devices, turns, first, *refs):
    refs = list(refs)
    turned_refs = [refs.pop(0) for _ in range(turns)]
    place_ref = refs.pop(0)
    message_ref, unit_ref = refs[:2]
    del refs[:2]
    level_ref = None if first else refs.pop(0)
    stat_ref = None if first and piece == 0 else refs.pop(0)
    flow_ref = refs.pop(0) if piece else None
    moved_ref, flow_out = refs[:2]
    del refs[:2]
    all_hours, quarter = moved_ref.shape
    if first:
        level_out = refs.pop(0)
        levels = starting_levels(piece, devices, place_ref[0], message_ref, all_hours, quarter)
        level_out[...] = levels
    else:
        levels = level_ref[...]
    if piece == 0:
        stat_out = refs.pop(0)
        if first:
            stat_out[...] = jnp.full(stat_out.shape, 1.0, FULL)
        else:
            dual_sq = total(message_ref[:all_hours, quarter:].astype(FULL))
            primal_sq = stat_ref[1:2, 0:1]
            ratio = (dual_sq + 1e-06) / (primal_sq + 1e-06)
            weight = jnp.sqrt(stat_ref[0:1, 0:1]) * jnp.sqrt(jnp.sqrt(ratio))
            stat_out[...] = jnp.broadcast_to(weight, stat_out.shape)
        stat_ref = stat_out
    half = primal_piece(piece, step_size, stat_ref, message_ref, levels, unit_ref, moved_ref)
    lines = turned_refs[0].shape[2]
    for k in range(turns * turned_refs[0].shape[0]):
        at = pl.ds(k * lines, lines)
        part = piece_flows(piece, half, turned_refs, k)
        flow_out[:, at] = part if flow_ref is None else flow_ref[:, at] + part


def dual_kernel(step_size, balance, devices, turns, first, last, *refs):
    refs = list(refs)
    turned_refs = [refs.pop(0) for _ in range(turns)]
    place_ref, masked_ref, message_ref = refs[:3]
    del refs[:3]
    level_refs = [refs.pop(0) for _ in range(3 if first else 4)]
    moved_refs = [refs.pop(0) for _ in range(3)]
    stat_ref, flow_ref, dual_ref, base_ref, rating_ref, unit_ref, cost_ref, demand_ref, ramp_ref = refs[:9]
    del refs[:9]
    price_ref = None if first else refs.pop(0)
    if first:
        level_refs.append(refs.pop())
    if last:
        level_out, dual_out, ramp_out, price_out, last_moved = refs
    else:
        last_moved, dual_out, ramp_out, price_out, stat_out, send_ref, half_dual, term_out = refs
    moved_refs = moved_refs + [last_moved]

    ctgs, lines, units = masked_ref.shape
    width, quarter = units // 2, units // 4
    all_hours, hours = level_refs[0].shape[0], cost_ref.shape[0]
    place = place_ref[0]
    first_hour = place * hours
    weight = stat_ref[0:1, 0:1]
    dual_step = step_size * weight

    if first:
        level_refs[3][...] = starting_levels(3, devices, place, message_ref, all_hours, quarter)
    half = primal_piece(3, step_size, stat_ref, message_ref, level_refs[3][...], unit_ref, last_moved)
    flow_acc = jnp.zeros((all_hours, lines), FULL)
    for k in range(ctgs):
        at = pl.ds(k * lines, lines)
        flows = flow_ref[:, at] + piece_flows(3, half, turned_refs, k)
        old = dual_ref[:, at]
        trial = old + dual_step * flows
        base, rating = base_ref[:, at], rating_ref[:, at]
        new = trial - jnp.clip(trial, dual_step * (base - rating), dual_step * (base + rating))
        if last:
            dual_out[:, k, :] = new
        else:
            dual_out[:, at] = new
            half_dual[:, at] = new.astype(HALF)
            flow_acc = flow_acc + (new - old) ** 2

    places = [pl.ds(piece_at(piece, units), quarter) for piece in range(PIECES)]
    moved_sq = None if last else total(flow_acc)
    supply = [jnp.zeros((1, 1), FULL) for _ in range(hours)]
    ramps = [[] for _ in range(hours)]
    for piece in range(PIECES):
        at = places[piece]
        ramp_limit, ramp_on = unit_ref[2:3, at], unit_ref[3:4, at]
        rows = []
        for j in range(hours + 1):
            spot = pl.ds(jnp.minimum(first_hour + j, all_hours - 1), 1)
            rows.append(2.0 * moved_refs[piece][spot, :] - level_refs[piece][spot, :])
        for j in range(hours):
            old = ramp_ref[j : j + 1, at]
            trial = old + dual_step * (ramp_on * (rows[j + 1] - rows[j]))
            reach = dual_step * ramp_limit
            new = trial - jnp.clip(trial, -reach, reach)
            supply[j] = supply[j] + jnp.sum(rows[j], axis=1, keepdims=True)
            ramps[j].append(new)
            if last:
                own = pl.multiple_of(own_first(place, piece % 2, width) + (piece // 2) * quarter, LANES)
                level_out[j : j + 1, pl.ds(own, quarter)] = moved_refs[piece][pl.ds(first_hour + j, 1), :]
                ramp_out[j : j + 1, pl.ds(own, quarter)] = new
            else:
                ramp_out[j : j + 1, at] = new
                moved_sq = moved_sq + total((new - old) ** 2)
    prices = []
    for j in range(hours):
        old = jnp.zeros((1, 1), FULL) if first else price_ref[j : j + 1, :]
        new = old + dual_step * (balance * (supply[j] - demand_ref[0:1, j : j + 1]))
        prices.append(balance * new)
        if last:
            price_out[j] = new[0, 0]
        else:
            price_out[j : j + 1, :] = new
            moved_sq = moved_sq + (new - old) ** 2
    if last:
        return

    primal_acc = jnp.zeros((all_hours, quarter), FULL)
    for piece in range(PIECES):
        primal_acc = primal_acc + (moved_refs[piece][...] - level_refs[piece][...]) ** 2
    row = lax.broadcasted_iota(jnp.int32, stat_out.shape, 0)
    stat_out[...] = jnp.where(row == 0, weight, total(primal_acc))
    for piece in range(PIECES):
        at = places[piece]
        terms = hour_terms(
            [cost_ref[j : j + 1, at] for j in range(hours)],
            [ramps[j][piece] for j in range(hours)],
            unit_ref[3:4, at],
            prices,
        )
        for j, term in enumerate(terms):
            term_out[j : j + 1, at] = term
    block = scalar_block(moved_sq, place, (all_hours, LANES))
    pull_piece(1, hours, first_hour, masked_ref, half_dual, term_out, send_ref)
    send_ref[:, quarter:] = block


def pull_piece(piece, hours, first_hour, masked_ref, half_dual, term_ref, out_ref):
    ctgs, lines, units = masked_ref.shape
    whole = masked_ref.reshape(ctgs * lines, units)
    for at in range(0, units // 4, WIDE):
        cols = pl.ds(piece_at(piece, units) + at, WIDE)
        pulled = jnp.dot(half_dual[...], whole[:, cols], preferred_element_type=FULL)
        terms = [term_ref[j : j + 1, cols] for j in range(hours + 1)]
        out_ref[:, pl.ds(at, WIDE)] = add_rows(pulled, first_hour, terms).astype(HALF)


def middle_pull_kernel(hours, place_ref, masked_ref, half_dual, term_ref, send_a, keep_a, send_b):
    quarter = send_b.shape[1]
    pull_piece(0, hours, place_ref[0] * hours, masked_ref, half_dual, term_ref, keep_a)
    keep_a[:, quarter:] = send_a[:, quarter:]
    pull_piece(3, hours, place_ref[0] * hours, masked_ref, half_dual, term_ref, send_b)


def last_pull_kernel(hours, place_ref, masked_ref, half_dual, term_ref, keep_b):
    pull_piece(2, hours, place_ref[0] * hours, masked_ref, half_dual, term_ref, keep_b)


def add_kernel(own_ref, received_ref, before_ref, out_ref):
    out_ref[...] = (own_ref[...].astype(FULL) + received_ref[...].astype(FULL)).astype(HALF)


def add_after(own, received, before):
    return call(add_kernel, "add", 0.1, [own, received, before], [near(*own.shape, dtype=HALF)])[0]


def join_kernel(all_hours, own_ref, received_ref, *refs):
    out_ref, scratch_ref = refs[-2:]
    extra = own_ref.shape[0] - all_hours
    own, received = own_ref[...].astype(FULL), received_ref[...].astype(FULL)
    scratch_ref[:all_hours, :] = own[:all_hours] + received[:all_hours]
    scratch_ref[all_hours : all_hours + extra, :] = own[all_hours:]
    scratch_ref[all_hours + extra :, :] = received[all_hours:]
    if out_ref is not None:
        out_ref[...] = scratch_ref[...].astype(HALF)


def split_kernel(all_hours, own_ref, received_ref, a_ref, b_ref, scratch_ref):
    join_kernel(all_hours, own_ref, received_ref, None, scratch_ref)
    quarter = b_ref.shape[1]
    a_ref[:, :quarter] = scratch_ref[:, :quarter].astype(HALF)
    a_ref[:, quarter:] = jnp.zeros((a_ref.shape[0], a_ref.shape[1] - quarter), HALF)
    b_ref[...] = scratch_ref[:, quarter:].astype(HALF)


def first_join(all_hours, own, received):
    rows, quarter = 2 * own.shape[0] - all_hours, own.shape[1] // 2
    return call(
        functools.partial(split_kernel, all_hours),
        "split",
        0.3,
        [own, received],
        [near(rows, quarter + LANES, dtype=HALF), near(rows, quarter, dtype=HALF)],
        [near(rows, 2 * quarter)],
    )


def join(all_hours, own, received, *before):
    shape = (2 * own.shape[0] - all_hours, own.shape[1])
    kernel = functools.partial(join_kernel, all_hours)
    return call(kernel, "join", 0.2, [own, received, *before], [near(*shape, dtype=HALF)], [near(*shape)])[0]


def exchange(x, mask):
    devices = lax.axis_size("ctg")
    flip = 0 if mask == 1 else 1
    return lax.ppermute(x, "ctg", [(i, i ^ mask ^ flip) for i in range(devices)])


def mask_order(devices, q, first):
    masks = [1 << b for b in range(1, devices.bit_length() - 1)]
    turn, back = ORDERS[(2 if first else 0) + q]
    masks = masks[turn:] + masks[:turn]
    return masks[::-1] if back else masks


def body(
    flow_tiles,
    tile_pattern,
    monitored,
    ratings,
    base_flow,
    unit_cost,
    unit_floor,
    unit_span,
    ramp_limit,
    ramp_mask,
    demand,
    start_output,
    start_flow_dual,
    start_ramp_dual,
):
    ctgs, lines, units = flow_tiles.shape
    all_hours, hours = start_flow_dual.shape[0], start_output.shape[0]
    devices = lax.axis_size("ctg")
    here = lax.axis_index("ctg").astype(jnp.int32).reshape(1)
    quarter = units // 4
    assert devices & (devices - 1) == 0 and 2 <= devices <= LANES and quarter % WIDE == 0
    step_size = 0.5 / (2.0 + math.sqrt(ctgs * devices * lines / units))
    balance = 1.0 / math.sqrt(units)
    spread = -ratings.shape[0] % (8 * LANES)
    table = jnp.pad(ratings, (0, spread)).reshape(-1, LANES)
    row = lambda x: x.reshape(1, units)
    start_rows = all_hours + 2 * hours
    start = near(start_rows, 2 * quarter, dtype=HALF)
    message_a, message_b = near(all_hours, quarter + LANES, dtype=HALF), near(all_hours, quarter, dtype=HALF)

    operands = [flow_tiles, start_flow_dual, row(ramp_mask), unit_cost, start_ramp_dual, start_output]
    masked, send, keep = pl.pallas_call(
        start_kernel,
        out_shape=(near(ctgs, lines, units, dtype=HALF), start, start),
        in_specs=[SMEM, HBM, HBM] + [VMEM] * 5,
        out_specs=(VMEM,) * 3,
        scratch_shapes=[
            pltpu.SMEM(tile_pattern.shape, jnp.int32),
            near(all_hours, units),
            pltpu.SemaphoreType.DMA((ctgs, 2)),
            pltpu.SemaphoreType.DMA,
        ],
        compiler_params=pltpu.CompilerParams(vmem_limit_bytes=46 * MIB),
        name="start",
    )(here, far(tile_pattern), *[far(x) for x in operands])
    masked = pltpu.with_memory_space_constraint(masked, pltpu.VMEM)
    demands = demand.reshape(1, hours)
    price, stat, levels, turned = None, None, None, []
    for iteration in range(ITERS):
        first, last = iteration == 0, iteration == ITERS - 1
        merge = functools.partial(join, all_hours) if first else jnp.add
        if first:
            owns = list(first_join(all_hours, keep, exchange(send, 1)))
        else:
            owns = [keep_a + exchange(send_a, 1), keep_b + exchange(send_b, 1)]
        orders = [mask_order(devices, q, first) for q in range(2)]
        steps = len(orders[0])
        for step in range(steps):
            before = []
            if first and step == steps - 1:
                operands = [start_flow_dual, base_flow, monitored, table, row(unit_floor), row(unit_span)]
                operands += [row(ramp_limit), row(ramp_mask), unit_cost, start_ramp_dual]
                dual, base, rating, unit, cost, ramp = call(
                    prepare_kernel,
                    "prepare",
                    1.5,
                    [here, owns[0], *[far(x) for x in operands]],
                    [
                        near(all_hours, ctgs * lines),
                        near(all_hours, ctgs * lines),
                        near(1, ctgs * lines),
                        near(4, units),
                        near(hours, units),
                        near(hours, units),
                    ],
                    smem=(0,),
                )
                before.append(rating)
            if first:
                share = [0] * (steps - len(TURNS)) + [ctgs * part // 8 for part in TURNS]
                for turn in range(sum(share[:step]), sum(share[: step + 1])):
                    turned += call(
                        functools.partial(turn_kernel, turn),
                        "turn",
                        0.45,
                        [masked, owns[0]],
                        [near(1, units, lines, dtype=HALF)],
                    )
                before += turned
            owns[0] = merge(owns[0], exchange(owns[0], orders[0][step]), *before)
            if first or step < steps - 1:
                owns[1] = merge(owns[1], exchange(owns[1], orders[1][step]))
        messages = [owns[0], exchange(owns[0], 1)]
        moved, flows = [], None
        levels = [] if first else levels
        for piece in range(3):
            if piece == 2:
                if not first:
                    owns[1] = add_after(owns[1], exchange(owns[1], orders[1][-1]), after)
                messages += [owns[1], exchange(owns[1], 1)]
            operands = [*turned, here, messages[piece], unit]
            operands += [] if first else [levels[piece]]
            operands += [] if first and piece == 0 else [stat]
            operands += [flows] if piece else []
            out_shape = [near(all_hours, quarter), near(all_hours, ctgs * lines)]
            out_shape += [near(all_hours, quarter)] if first else []
            out_shape += [] if piece else [near(8, LANES)]
            kernel = functools.partial(flow_kernel, step_size, piece, devices, len(turned), first)
            outs = call(kernel, "flow", 0.7, operands, out_shape, smem=(len(turned),))
            moved.append(outs[0])
            flows = outs[1]
            if first:
                levels.append(outs[2])
            if piece == 0:
                stat = after = outs[-1]
        operands = [*turned, here, masked, messages[3], *levels, *moved, stat, flows, dual, base, rating, unit, cost]
        operands += [demands, ramp] if first else [demands, ramp, price]
        kernel = functools.partial(dual_kernel, step_size, balance, devices, len(turned), first, last)
        smem = (len(turned),)
        if last:
            f32 = lambda *shape: jax.ShapeDtypeStruct(shape, FULL)
            out_shape = [f32(hours, units), f32(all_hours, ctgs, lines), f32(hours, units), f32(hours)]
            return call(kernel, "dual", 1.2, operands, out_shape, [near(all_hours, quarter)], smem, (3,))
        out_shape = [near(all_hours, quarter), near(all_hours, ctgs * lines), near(hours, units), near(hours, 1)]
        out_shape += [near(8, LANES), message_a, near(all_hours, ctgs * lines, dtype=HALF), near(8, units)]
        scratch = [near(all_hours, quarter)] if first else []
        outs = call(kernel, "dual", 1.5, operands, out_shape, scratch, smem)
        levels = (*moved, outs[0])
        dual, ramp, price, stat, send_a, half_dual, terms = outs[1:]
        operands = [here, masked, half_dual, terms]
        keep_a, send_b = call(
            functools.partial(middle_pull_kernel, hours),
            "pull",
            1.2,
            [*operands, send_a],
            [message_a, message_b],
            smem=(0,),
        )
        (keep_b,) = call(functools.partial(last_pull_kernel, hours), "pull", 0.6, operands, [message_b], smem=(0,))


def solution(mesh):
    return jax.shard_map(
        body,
        mesh=mesh,
        in_specs=(
            P("ctg", None, None),
            P("ctg", None, None),
            P("ctg", None),
            P(),
            P("grp", "ctg", None),
            P(("grp", "ctg"), None),
            P(),
            P(),
            P(),
            P(),
            P(("grp", "ctg")),
            P(("grp", "ctg"), None),
            P("grp", "ctg", None),
            P(("grp", "ctg"), None),
        ),
        out_specs=(
            P(("grp", "ctg"), None),
            P("grp", "ctg", None),
            P(("grp", "ctg"), None),
            P(("grp", "ctg")),
        ),
        check_vma=False,
    )
```

```python
import functools
import math

import jax
import jax.numpy as jnp
from jax import lax
from jax.experimental import pallas as pl
from jax.experimental.pallas import tpu as pltpu
from jax.sharding import PartitionSpec as P

ITERS = 4
LANES = 128
WIDE = 256
MIB = 2**20
HALF = jnp.bfloat16
FULL = jnp.float32

PIECES = 4
TURNS = (0, 4, 4)
ORDERS = ((0, 0), (2, 0), (1, 0), (2, 0))

VMEM = pl.BlockSpec(memory_space=pltpu.VMEM)
SMEM = pl.BlockSpec(memory_space=pltpu.SMEM)
HBM = pl.BlockSpec(memory_space=pltpu.HBM)


def near(*shape, dtype=FULL):
    return pltpu.VMEM(shape, dtype)


def far(x):
    return pltpu.with_memory_space_constraint(x, pltpu.HBM)


def call(kernel, name, us, operands, out_shape, scratch=(), smem=(), smem_out=(), limit=12):
    outs = pl.pallas_call(
        kernel,
        out_shape=tuple(out_shape),
        in_specs=[SMEM if j in smem else VMEM for j in range(len(operands))],
        out_specs=tuple(SMEM if j in smem_out else VMEM for j in range(len(out_shape))),
        scratch_shapes=list(scratch),
        compiler_params=pltpu.CompilerParams(vmem_limit_bytes=limit * MIB),
        cost_estimate=pl.CostEstimate(flops=0, bytes_accessed=int(us * 3.69e6), transcendentals=0),
        name=name,
    )(*operands)
    return list(outs)


def total(x):
    return jnp.sum(jnp.sum(x, axis=1, keepdims=True), axis=0, keepdims=True)


def piece_at(piece, units):
    return (piece % 2) * (units // 2) + (piece // 2) * (units // 4)


def parity(index):
    odd = index % 2
    for bit in range(1, LANES.bit_length() - 1):
        odd = odd ^ ((index // 2**bit) % 2)
    return odd


def own_first(place, s, width):
    side = parity(place)
    return pl.multiple_of((side if s == 0 else 1 - side) * width, LANES)


def add_rows(values, first, rows):
    row = lax.broadcasted_iota(jnp.int32, values.shape, 0)
    for j, extra in enumerate(rows):
        values = values + jnp.where(row == first + j, extra, 0.0)
    return values


def hour_terms(cost, ramp, on, price_terms):
    hours = len(cost)
    rows = []
    for j in range(hours + 1):
        if j == hours:
            rows.append(on * ramp[j - 1])
            continue
        row = cost[j] + on * ((ramp[j - 1] if j else 0.0) - ramp[j])
        if price_terms is not None:
            row = row + price_terms[j]
        rows.append(row)
    return rows


def scalar_block(value, place, shape):
    row = lax.broadcasted_iota(jnp.int32, shape, 0)
    lane = lax.broadcasted_iota(jnp.int32, shape, 1)
    block = jnp.zeros(shape, FULL)
    left = value
    for j in range(3):
        part = left.astype(HALF).astype(FULL)
        left = left - part
        block = block + jnp.where((row == j) & (lane == place), part, 0.0)
    return block.astype(HALF)


def start_kernel(
    place_ref,
    gate_hbm,
    tiles_ref,
    dual_ref,
    on_ref,
    cost_ref,
    ramp_ref,
    level_ref,
    masked_ref,
    send_ref,
    keep_ref,
    gate_ref,
    acc_ref,
    sems,
    gate_sem,
):
    ctgs, lines, units = masked_ref.shape
    width, quarter = units // 2, units // 4
    half_tiles = width // LANES
    all_hours, hours = dual_ref.shape[0], cost_ref.shape[0]
    place = place_ref[0]

    def copy(k, s):
        return pltpu.make_async_copy(
            tiles_ref.at[k, :, pl.ds(own_first(place, s, width), width)],
            masked_ref.at[k, :, pl.ds(s * width, width)],
            sems.at[k, s],
        )

    gates = pltpu.make_async_copy(gate_hbm, gate_ref, gate_sem)
    gates.start()
    for k in range(ctgs):
        for s in range(2):
            copy(k, s).start()

    gates.wait()
    for k in range(ctgs):
        lhs = dual_ref[:, k, :].astype(HALF)
        for s in range(2):
            copy(k, s).wait()
            gate_at = own_first(place, s, width) // LANES
            for j in range(0, half_tiles, 2):
                at = s * width + j * LANES
                block = []
                for m in range(lines // LANES):
                    line = []
                    for i in range(2):
                        gate = gate_ref[k, m, gate_at + j + i]
                        part = masked_ref[k, pl.ds(m * LANES, LANES), pl.ds(at + i * LANES, LANES)]
                        line.append(jnp.where(gate > 0, part, jnp.zeros((), HALF)))
                    block.append(jnp.concatenate(line, axis=1))
                block = jnp.concatenate(block, axis=0)
                cols = pl.ds(at, WIDE)
                masked_ref[k, :, cols] = block
                part = jnp.dot(lhs, block, preferred_element_type=FULL)
                acc_ref[:, cols] = part if k == 0 else acc_ref[:, cols] + part

    for s, out_ref in enumerate((keep_ref, send_ref)):
        message = []
        for piece in (s, 2 + s):
            cols = pl.ds(piece_at(piece, units), quarter)
            own = pl.ds(pl.multiple_of(own_first(place, s, width) + (piece // 2) * quarter, LANES), quarter)
            rows = hour_terms(
                [cost_ref[j : j + 1, own] for j in range(hours)],
                [ramp_ref[j : j + 1, own] for j in range(hours)],
                on_ref[:, own].astype(FULL),
                None,
            )
            values = add_rows(acc_ref[:, cols], place * hours, rows)
            level = level_ref[:, own]
            high = level.astype(HALF).astype(FULL)
            message.append(jnp.concatenate([values, high, level - high], axis=0))
        out_ref[...] = jnp.concatenate(message, axis=1).astype(HALF)


def prepare_kernel(
    place_ref,
    before_ref,
    dual_ref,
    base_ref,
    monitored_ref,
    ratings_ref,
    floor_ref,
    span_ref,
    limit_ref,
    on_ref,
    cost_ref,
    ramp_ref,
    dual_out,
    base_out,
    rating_out,
    unit_out,
    cost_out,
    ramp_out,
):
    ctgs, lines = monitored_ref.shape
    width = floor_ref.shape[1] // 2
    place = place_ref[0]
    table = ratings_ref[...].T
    hi = table.astype(HALF)
    left = table - hi.astype(FULL)
    mid = left.astype(HALF)
    lo = (left - mid.astype(FULL)).astype(HALF)
    groups = table.shape[1]
    for k in range(ctgs):
        cols = pl.ds(k * lines, lines)
        dual_out[:, cols] = dual_ref[:, k, :]
        base_out[:, cols] = base_ref[:, k, :]
        index = monitored_ref[k : k + 1, :]
        group = lax.broadcasted_iota(jnp.int32, (groups, lines), 0)
        chosen = (group == index // LANES).astype(FULL).astype(HALF)
        picked = (
            jnp.dot(hi, chosen, preferred_element_type=FULL)
            + jnp.dot(mid, chosen, preferred_element_type=FULL)
            + jnp.dot(lo, chosen, preferred_element_type=FULL)
        )
        lane = lax.broadcasted_iota(jnp.int32, (LANES, lines), 0)
        rating_out[:, cols] = jnp.sum(jnp.where(lane == index % LANES, picked, 0.0), axis=0, keepdims=True)
    for s in range(2):
        cols, own = pl.ds(s * width, width), pl.ds(own_first(place, s, width), width)
        floor = floor_ref[:, own]
        unit_out[0:1, cols] = floor
        unit_out[1:2, cols] = floor + span_ref[:, own]
        unit_out[2:3, cols] = limit_ref[:, own]
        unit_out[3:4, cols] = on_ref[:, own].astype(FULL)
        cost_out[:, cols] = cost_ref[:, own]
        ramp_out[:, cols] = ramp_ref[:, own]


def turn_kernel(first_ctg, masked_ref, before_ref, out_ref):
    ctgs, units, lines = out_ref.shape
    for k in range(ctgs):
        for at in range(0, units, WIDE):
            out_ref[k, pl.ds(at, WIDE), :] = masked_ref[first_ctg + k, :, pl.ds(at, WIDE)].T


def starting_levels(piece, devices, place, message_ref, all_hours, quarter):
    hours = all_hours // devices
    levels = message_ref[all_hours:, :quarter]
    shape = (all_hours, levels.shape[0])
    hour = lax.broadcasted_iota(jnp.int32, shape, 0)
    row = lax.broadcasted_iota(jnp.int32, shape, 1)
    apart = place ^ (hour // hours) ^ (piece % 2)
    block = parity(apart)
    for bit, mask in enumerate(mask_order(devices, piece // 2, True)):
        block = block + ((apart // mask) % 2) * 2 ** (bit + 1)
    chosen = (row // (2 * hours) == block) & (row % hours == hour % hours)
    return jnp.dot(chosen.astype(FULL).astype(HALF), levels, preferred_element_type=FULL)


def primal_piece(piece, step_size, stat_ref, message_ref, levels, unit_ref, moved_ref):
    all_hours, quarter = levels.shape
    cols = pl.ds(piece_at(piece, unit_ref.shape[1]), quarter)
    primal_step = step_size / stat_ref[0:1, 0:1]
    gradient = message_ref[:all_hours, :quarter].astype(FULL)
    moved = jnp.clip(levels - primal_step * gradient, unit_ref[0:1, cols], unit_ref[1:2, cols])
    moved_ref[...] = moved
    return (2.0 * moved - levels).astype(HALF)


def piece_flows(piece, half, turned_refs, k):
    turned_ref = turned_refs[k // turned_refs[0].shape[0]]
    rows = pl.ds(piece_at(piece, turned_ref.shape[1]), half.shape[1])
    return jnp.dot(half, turned_ref[k % turned_refs[0].shape[0], rows, :], preferred_element_type=FULL)


def flow_kernel(step_size, pieces, devices, turns, first, *refs):
    refs = list(refs)
    turned_refs = [refs.pop(0) for _ in range(turns)]
    place_ref, unit_ref = refs[:2]
    del refs[:2]
    leading = pieces[0] == 0
    stat_ref = None if first and leading else refs.pop(0)
    flow_ref = None if leading else refs.pop(0)
    message_refs = [refs.pop(0) for _ in pieces]
    level_refs = [refs.pop(0) for _ in pieces]
    moved_refs = [refs.pop(0) for _ in pieces]
    flow_out = refs.pop(0)
    all_hours, quarter = moved_refs[0].shape
    if leading:
        stat_out = refs.pop(0)
        if first:
            stat_out[...] = jnp.full(stat_out.shape, 1.0, FULL)
        else:
            dual_sq = total(message_refs[0][:all_hours, quarter:].astype(FULL))
            primal_sq = stat_ref[1:2, 0:1]
            ratio = (dual_sq + 1e-06) / (primal_sq + 1e-06)
            weight = jnp.sqrt(stat_ref[0:1, 0:1]) * jnp.sqrt(jnp.sqrt(ratio))
            stat_out[...] = jnp.broadcast_to(weight, stat_out.shape)
        stat_ref = stat_out
    halves = []
    for piece, message_ref, level_ref, moved_ref in zip(pieces, message_refs, level_refs, moved_refs):
        if first:
            level_ref[...] = starting_levels(piece, devices, place_ref[0], message_ref, all_hours, quarter)
        halves.append(primal_piece(piece, step_size, stat_ref, message_ref, level_ref[...], unit_ref, moved_ref))
    lines = turned_refs[0].shape[2]
    for k in range(turns * turned_refs[0].shape[0]):
        at = pl.ds(k * lines, lines)
        part = None if flow_ref is None else flow_ref[:, at]
        for piece, half in zip(pieces, halves):
            flows = piece_flows(piece, half, turned_refs, k)
            part = flows if part is None else part + flows
        flow_out[:, at] = part


def dual_kernel(step_size, balance, devices, turns, first, last, *refs):
    refs = list(refs)
    turned_refs = [refs.pop(0) for _ in range(turns)]
    place_ref, masked_ref, message_ref = refs[:3]
    del refs[:3]
    level_refs = [refs.pop(0) for _ in range(3 if first else 4)]
    moved_refs = [refs.pop(0) for _ in range(3)]
    stat_ref, flow_ref, dual_ref, base_ref, rating_ref, unit_ref, cost_ref, demand_ref, ramp_ref = refs[:9]
    del refs[:9]
    price_ref = None if first else refs.pop(0)
    if first:
        level_refs.append(refs.pop())
    if last:
        level_out, dual_out, ramp_out, price_out, last_moved = refs
    else:
        last_moved, dual_out, ramp_out, price_out, stat_out, send_ref, half_dual, term_out = refs
    moved_refs = moved_refs + [last_moved]

    ctgs, lines, units = masked_ref.shape
    width, quarter = units // 2, units // 4
    all_hours, hours = level_refs[0].shape[0], cost_ref.shape[0]
    place = place_ref[0]
    first_hour = place * hours
    weight = stat_ref[0:1, 0:1]
    dual_step = step_size * weight

    if first:
        level_refs[3][...] = starting_levels(3, devices, place, message_ref, all_hours, quarter)
    half = primal_piece(3, step_size, stat_ref, message_ref, level_refs[3][...], unit_ref, last_moved)
    flow_acc = jnp.zeros((all_hours, lines), FULL)
    for k in range(ctgs):
        at = pl.ds(k * lines, lines)
        flows = flow_ref[:, at] + piece_flows(3, half, turned_refs, k)
        old = dual_ref[:, at]
        trial = old + dual_step * flows
        base, rating = base_ref[:, at], rating_ref[:, at]
        new = trial - jnp.clip(trial, dual_step * (base - rating), dual_step * (base + rating))
        if last:
            dual_out[:, k, :] = new
        else:
            dual_out[:, at] = new
            half_dual[:, at] = new.astype(HALF)
            flow_acc = flow_acc + (new - old) ** 2

    places = [pl.ds(piece_at(piece, units), quarter) for piece in range(PIECES)]
    moved_sq = None if last else total(flow_acc)
    supply = [jnp.zeros((1, 1), FULL) for _ in range(hours)]
    ramps = [[] for _ in range(hours)]
    for piece in range(PIECES):
        at = places[piece]
        ramp_limit, ramp_on = unit_ref[2:3, at], unit_ref[3:4, at]
        rows = []
        for j in range(hours + 1):
            spot = pl.ds(jnp.minimum(first_hour + j, all_hours - 1), 1)
            rows.append(2.0 * moved_refs[piece][spot, :] - level_refs[piece][spot, :])
        for j in range(hours):
            old = ramp_ref[j : j + 1, at]
            trial = old + dual_step * (ramp_on * (rows[j + 1] - rows[j]))
            reach = dual_step * ramp_limit
            new = trial - jnp.clip(trial, -reach, reach)
            supply[j] = supply[j] + jnp.sum(rows[j], axis=1, keepdims=True)
            ramps[j].append(new)
            if last:
                own = pl.multiple_of(own_first(place, piece % 2, width) + (piece // 2) * quarter, LANES)
                level_out[j : j + 1, pl.ds(own, quarter)] = moved_refs[piece][pl.ds(first_hour + j, 1), :]
                ramp_out[j : j + 1, pl.ds(own, quarter)] = new
            else:
                ramp_out[j : j + 1, at] = new
                moved_sq = moved_sq + total((new - old) ** 2)
    prices = []
    for j in range(hours):
        old = jnp.zeros((1, 1), FULL) if first else price_ref[j : j + 1, :]
        new = old + dual_step * (balance * (supply[j] - demand_ref[0:1, j : j + 1]))
        prices.append(balance * new)
        if last:
            price_out[j] = new[0, 0]
        else:
            price_out[j : j + 1, :] = new
            moved_sq = moved_sq + (new - old) ** 2
    if last:
        return

    primal_acc = jnp.zeros((all_hours, quarter), FULL)
    for piece in range(PIECES):
        primal_acc = primal_acc + (moved_refs[piece][...] - level_refs[piece][...]) ** 2
    row = lax.broadcasted_iota(jnp.int32, stat_out.shape, 0)
    stat_out[...] = jnp.where(row == 0, weight, total(primal_acc))
    for piece in range(PIECES):
        at = places[piece]
        terms = hour_terms(
            [cost_ref[j : j + 1, at] for j in range(hours)],
            [ramps[j][piece] for j in range(hours)],
            unit_ref[3:4, at],
            prices,
        )
        for j, term in enumerate(terms):
            term_out[j : j + 1, at] = term
    block = scalar_block(moved_sq, place, (all_hours, LANES))
    pull_piece(1, hours, first_hour, masked_ref, half_dual, term_out, send_ref)
    send_ref[:, quarter:] = block


def pull_piece(piece, hours, first_hour, masked_ref, half_dual, term_ref, out_ref):
    ctgs, lines, units = masked_ref.shape
    whole = masked_ref.reshape(ctgs * lines, units)
    for at in range(0, units // 4, WIDE):
        cols = pl.ds(piece_at(piece, units) + at, WIDE)
        pulled = jnp.dot(half_dual[...], whole[:, cols], preferred_element_type=FULL)
        terms = [term_ref[j : j + 1, cols] for j in range(hours + 1)]
        out_ref[:, pl.ds(at, WIDE)] = add_rows(pulled, first_hour, terms).astype(HALF)


def middle_pull_kernel(hours, place_ref, masked_ref, half_dual, term_ref, send_a, keep_a, send_b):
    quarter = send_b.shape[1]
    pull_piece(0, hours, place_ref[0] * hours, masked_ref, half_dual, term_ref, keep_a)
    keep_a[:, quarter:] = send_a[:, quarter:]
    pull_piece(3, hours, place_ref[0] * hours, masked_ref, half_dual, term_ref, send_b)


def last_pull_kernel(hours, place_ref, masked_ref, half_dual, term_ref, keep_b):
    pull_piece(2, hours, place_ref[0] * hours, masked_ref, half_dual, term_ref, keep_b)


def add_kernel(own_ref, received_ref, before_ref, out_ref):
    out_ref[...] = (own_ref[...].astype(FULL) + received_ref[...].astype(FULL)).astype(HALF)


def add_after(own, received, before):
    return call(add_kernel, "add", 0.1, [own, received, before], [near(*own.shape, dtype=HALF)])[0]


def join_kernel(all_hours, own_ref, received_ref, *refs):
    out_ref, scratch_ref = refs[-2:]
    extra = own_ref.shape[0] - all_hours
    own, received = own_ref[...].astype(FULL), received_ref[...].astype(FULL)
    scratch_ref[:all_hours, :] = own[:all_hours] + received[:all_hours]
    scratch_ref[all_hours : all_hours + extra, :] = own[all_hours:]
    scratch_ref[all_hours + extra :, :] = received[all_hours:]
    if out_ref is not None:
        out_ref[...] = scratch_ref[...].astype(HALF)


def split_kernel(all_hours, own_ref, received_ref, a_ref, b_ref, scratch_ref):
    join_kernel(all_hours, own_ref, received_ref, None, scratch_ref)
    quarter = b_ref.shape[1]
    a_ref[...] = scratch_ref[:, :quarter].astype(HALF)
    b_ref[...] = scratch_ref[:, quarter:].astype(HALF)


def first_join(all_hours, own, received):
    rows, quarter = 2 * own.shape[0] - all_hours, own.shape[1] // 2
    return call(
        functools.partial(split_kernel, all_hours),
        "split",
        0.3,
        [own, received],
        [near(rows, quarter, dtype=HALF)] * 2,
        [near(rows, 2 * quarter)],
    )


def join(all_hours, own, received, *before):
    shape = (2 * own.shape[0] - all_hours, own.shape[1])
    kernel = functools.partial(join_kernel, all_hours)
    return call(kernel, "join", 0.2, [own, received, *before], [near(*shape, dtype=HALF)], [near(*shape)])[0]


def exchange(x, mask):
    devices = lax.axis_size("ctg")
    flip = 0 if mask == 1 else 1
    return lax.ppermute(x, "ctg", [(i, i ^ mask ^ flip) for i in range(devices)])


def mask_order(devices, q, first):
    masks = [1 << b for b in range(1, devices.bit_length() - 1)]
    turn, back = ORDERS[(2 if first else 0) + q]
    masks = masks[turn:] + masks[:turn]
    return masks[::-1] if back else masks


def body(
    flow_tiles,
    tile_pattern,
    monitored,
    ratings,
    base_flow,
    unit_cost,
    unit_floor,
    unit_span,
    ramp_limit,
    ramp_mask,
    demand,
    start_output,
    start_flow_dual,
    start_ramp_dual,
):
    ctgs, lines, units = flow_tiles.shape
    all_hours, hours = start_flow_dual.shape[0], start_output.shape[0]
    devices = lax.axis_size("ctg")
    here = lax.axis_index("ctg").astype(jnp.int32).reshape(1)
    quarter = units // 4
    assert devices & (devices - 1) == 0 and 2 <= devices <= LANES and quarter % WIDE == 0
    step_size = 0.5 / (2.0 + math.sqrt(ctgs * devices * lines / units))
    balance = 1.0 / math.sqrt(units)
    spread = -ratings.shape[0] % (8 * LANES)
    table = jnp.pad(ratings, (0, spread)).reshape(-1, LANES)
    row = lambda x: x.reshape(1, units)
    start_rows = all_hours + 2 * hours
    start = near(start_rows, 2 * quarter, dtype=HALF)
    message_a, message_b = near(all_hours, quarter + LANES, dtype=HALF), near(all_hours, quarter, dtype=HALF)

    operands = [flow_tiles, start_flow_dual, row(ramp_mask), unit_cost, start_ramp_dual, start_output]
    masked, send, keep = pl.pallas_call(
        start_kernel,
        out_shape=(near(ctgs, lines, units, dtype=HALF), start, start),
        in_specs=[SMEM, HBM, HBM] + [VMEM] * 5,
        out_specs=(VMEM,) * 3,
        scratch_shapes=[
            pltpu.SMEM(tile_pattern.shape, jnp.int32),
            near(all_hours, units),
            pltpu.SemaphoreType.DMA((ctgs, 2)),
            pltpu.SemaphoreType.DMA,
        ],
        compiler_params=pltpu.CompilerParams(vmem_limit_bytes=46 * MIB),
        name="start",
    )(here, far(tile_pattern), *[far(x) for x in operands])
    masked = pltpu.with_memory_space_constraint(masked, pltpu.VMEM)
    demands = demand.reshape(1, hours)
    price, stat, levels, turned = None, None, None, []
    for iteration in range(ITERS):
        first, last = iteration == 0, iteration == ITERS - 1
        merge = functools.partial(join, all_hours) if first else jnp.add
        if first:
            owns = list(first_join(all_hours, keep, exchange(send, 1)))
        else:
            owns = [keep_a + exchange(send_a, 1), keep_b + exchange(send_b, 1)]
        orders = [mask_order(devices, q, first) for q in range(2)]
        steps = len(orders[0])
        for step in range(steps):
            before = []
            if first and step == steps - 2:
                operands = [start_flow_dual, base_flow, monitored, table, row(unit_floor), row(unit_span)]
                operands += [row(ramp_limit), row(ramp_mask), unit_cost, start_ramp_dual]
                dual, base, rating, unit, cost, ramp = call(
                    prepare_kernel,
                    "prepare",
                    1.5,
                    [here, owns[0], *[far(x) for x in operands]],
                    [
                        near(all_hours, ctgs * lines),
                        near(all_hours, ctgs * lines),
                        near(1, ctgs * lines),
                        near(4, units),
                        near(hours, units),
                        near(hours, units),
                    ],
                    smem=(0,),
                )
                before.append(rating)
            if first:
                share = [0] * (steps - len(TURNS)) + [ctgs * part // 8 for part in TURNS]
                for turn in range(sum(share[:step]), sum(share[: step + 1])):
                    turned += call(
                        functools.partial(turn_kernel, turn),
                        "turn",
                        0.45,
                        [masked, owns[0]],
                        [near(1, units, lines, dtype=HALF)],
                    )
                before += turned
            owns[0] = merge(owns[0], exchange(owns[0], orders[0][step]), *before)
            if first or step < steps - 1:
                owns[1] = merge(owns[1], exchange(owns[1], orders[1][step]))
        messages = [owns[0], exchange(owns[0], 1)]
        moved, flows = [], None
        levels = [] if first else levels
        for pieces in ((0,), (1, 2)):
            if 2 in pieces:
                if not first:
                    owns[1] = add_after(owns[1], exchange(owns[1], orders[1][-1]), stat)
                messages += [owns[1], exchange(owns[1], 1)]
            operands = [*turned, here, unit]
            operands += [] if first and flows is None else [stat]
            operands += [] if flows is None else [flows]
            operands += [messages[piece] for piece in pieces]
            operands += [] if first else [levels[piece] for piece in pieces]
            out_shape = [near(all_hours, quarter)] * (len(pieces) * (2 if first else 1))
            out_shape += [near(all_hours, ctgs * lines)]
            out_shape += [near(8, LANES)] if flows is None else []
            kernel = functools.partial(flow_kernel, step_size, pieces, devices, len(turned), first)
            outs = call(kernel, "flow", 0.7 * len(pieces), operands, out_shape, smem=(len(turned),))
            if flows is None:
                stat = outs.pop()
            flows = outs.pop()
            if first:
                levels += outs[: len(pieces)]
            moved += outs[-len(pieces) :]
        operands = [*turned, here, masked, messages[3], *levels, *moved, stat, flows, dual, base, rating, unit, cost]
        operands += [demands, ramp] if first else [demands, ramp, price]
        kernel = functools.partial(dual_kernel, step_size, balance, devices, len(turned), first, last)
        smem = (len(turned),)
        if last:
            f32 = lambda *shape: jax.ShapeDtypeStruct(shape, FULL)
            out_shape = [f32(hours, units), f32(all_hours, ctgs, lines), f32(hours, units), f32(hours)]
            return tuple(call(kernel, "dual", 1.2, operands, out_shape, [near(all_hours, quarter)], smem, (3,)))
        out_shape = [near(all_hours, quarter), near(all_hours, ctgs * lines), near(hours, units), near(hours, 1)]
        out_shape += [near(8, LANES), message_a, near(all_hours, ctgs * lines, dtype=HALF), near(8, units)]
        scratch = [near(all_hours, quarter)] if first else []
        outs = call(kernel, "dual", 1.5, operands, out_shape, scratch, smem)
        levels = (*moved, outs[0])
        dual, ramp, price, stat, send_a, half_dual, terms = outs[1:]
        operands = [here, masked, half_dual, terms]
        keep_a, send_b = call(
            functools.partial(middle_pull_kernel, hours),
            "pull",
            1.2,
            [*operands, send_a],
            [message_a, message_b],
            smem=(0,),
        )
        (keep_b,) = call(functools.partial(last_pull_kernel, hours), "pull", 0.6, operands, [message_b], smem=(0,))


def solution(mesh):
    return jax.shard_map(
        body,
        mesh=mesh,
        in_specs=(
            P("ctg", None, None),
            P("ctg", None, None),
            P("ctg", None),
            P(),
            P("grp", "ctg", None),
            P(("grp", "ctg"), None),
            P(),
            P(),
            P(),
            P(),
            P(("grp", "ctg")),
            P(("grp", "ctg"), None),
            P("grp", "ctg", None),
            P(("grp", "ctg"), None),
        ),
        out_specs=(
            P(("grp", "ctg"), None),
            P("grp", "ctg", None),
            P(("grp", "ctg"), None),
            P(("grp", "ctg")),
        ),
        check_vma=False,
    )
```

```python
import functools
import math

import jax
import jax.numpy as jnp
from jax import lax
from jax.experimental import pallas as pl
from jax.experimental.pallas import tpu as pltpu
from jax.sharding import PartitionSpec as P

ITERS = 4
LANES = 128
WIDE = 256
MIB = 2**20
HALF = jnp.bfloat16
FULL = jnp.float32

PIECES = 4
SUMMANDS = 16
TURNS = (0, 4, 4)
ORDERS = ((2, 1), (0, 1), (1, 0), (2, 0))

VMEM = pl.BlockSpec(memory_space=pltpu.VMEM)
SMEM = pl.BlockSpec(memory_space=pltpu.SMEM)
HBM = pl.BlockSpec(memory_space=pltpu.HBM)


def near(*shape, dtype=FULL):
    return pltpu.VMEM(shape, dtype)


def far(x):
    return pltpu.with_memory_space_constraint(x, pltpu.HBM)


def call(kernel, name, us, operands, out_shape, scratch=(), smem=(), smem_out=(), limit=12):
    outs = pl.pallas_call(
        kernel,
        out_shape=tuple(out_shape),
        in_specs=[SMEM if j in smem else VMEM for j in range(len(operands))],
        out_specs=tuple(SMEM if j in smem_out else VMEM for j in range(len(out_shape))),
        scratch_shapes=list(scratch),
        compiler_params=pltpu.CompilerParams(vmem_limit_bytes=limit * MIB),
        cost_estimate=pl.CostEstimate(flops=0, bytes_accessed=int(us * 3.69e6), transcendentals=0),
        name=name,
    )(*operands)
    return list(outs)


def total(x):
    return jnp.sum(jnp.sum(x, axis=1, keepdims=True), axis=0, keepdims=True)


def piece_at(piece, units):
    return (piece % 2) * (units // 2) + (piece // 2) * (units // 4)


def parity(index):
    odd = index % 2
    for bit in range(1, LANES.bit_length() - 1):
        odd = odd ^ ((index // 2**bit) % 2)
    return odd


def own_first(place, s, width):
    side = parity(place)
    return pl.multiple_of((side if s == 0 else 1 - side) * width, LANES)


def add_rows(values, first, rows):
    row = lax.broadcasted_iota(jnp.int32, values.shape, 0)
    for j, extra in enumerate(rows):
        values = values + jnp.where(row == first + j, extra, 0.0)
    return values


def hour_terms(cost, ramp, on, price_terms):
    hours = len(cost)
    rows = []
    for j in range(hours + 1):
        if j == hours:
            rows.append(on * ramp[j - 1])
            continue
        row = cost[j] + on * ((ramp[j - 1] if j else 0.0) - ramp[j])
        if price_terms is not None:
            row = row + price_terms[j]
        rows.append(row)
    return rows


def scalar_block(value, place, shape):
    row = lax.broadcasted_iota(jnp.int32, shape, 0)
    lane = lax.broadcasted_iota(jnp.int32, shape, 1)
    block = jnp.zeros(shape, FULL)
    left = value
    for j in range(3):
        part = left.astype(HALF).astype(FULL)
        left = left - part
        block = block + jnp.where((row == j) & (lane == place), part, 0.0)
    return block.astype(HALF)


def start_kernel(
    place_ref,
    gate_hbm,
    tiles_ref,
    dual_ref,
    on_ref,
    cost_ref,
    ramp_ref,
    level_ref,
    masked_ref,
    send_ref,
    keep_ref,
    gate_ref,
    acc_ref,
    sems,
    gate_sem,
):
    ctgs, lines, units = masked_ref.shape
    width, quarter = units // 2, units // 4
    half_tiles = width // LANES
    all_hours, hours = dual_ref.shape[0], cost_ref.shape[0]
    place = place_ref[0]

    def copy(k, s):
        return pltpu.make_async_copy(
            tiles_ref.at[k, :, pl.ds(own_first(place, s, width), width)],
            masked_ref.at[k, :, pl.ds(s * width, width)],
            sems.at[k, s],
        )

    gates = pltpu.make_async_copy(gate_hbm, gate_ref, gate_sem)
    gates.start()
    for k in range(ctgs):
        for s in range(2):
            copy(k, s).start()

    gates.wait()
    for k in range(ctgs):
        lhs = dual_ref[:, k, :].astype(HALF)
        for s in range(2):
            copy(k, s).wait()
            gate_at = own_first(place, s, width) // LANES
            for j in range(0, half_tiles, 2):
                at = s * width + j * LANES
                block = []
                for m in range(lines // LANES):
                    line = []
                    for i in range(2):
                        gate = gate_ref[k, m, gate_at + j + i]
                        part = masked_ref[k, pl.ds(m * LANES, LANES), pl.ds(at + i * LANES, LANES)]
                        line.append(jnp.where(gate > 0, part, jnp.zeros((), HALF)))
                    block.append(jnp.concatenate(line, axis=1))
                block = jnp.concatenate(block, axis=0)
                cols = pl.ds(at, WIDE)
                masked_ref[k, :, cols] = block
                part = jnp.dot(lhs, block, preferred_element_type=FULL)
                acc_ref[:, cols] = part if k == 0 else acc_ref[:, cols] + part

    for s, out_ref in enumerate((keep_ref, send_ref)):
        message = []
        for piece in (s, 2 + s):
            cols = pl.ds(piece_at(piece, units), quarter)
            own = pl.ds(pl.multiple_of(own_first(place, s, width) + (piece // 2) * quarter, LANES), quarter)
            rows = hour_terms(
                [cost_ref[j : j + 1, own] for j in range(hours)],
                [ramp_ref[j : j + 1, own] for j in range(hours)],
                on_ref[:, own].astype(FULL),
                None,
            )
            values = add_rows(acc_ref[:, cols], place * hours, rows)
            level = level_ref[:, own]
            high = level.astype(HALF).astype(FULL)
            message.append(jnp.concatenate([values, high, level - high], axis=0))
        out_ref[...] = jnp.concatenate(message, axis=1).astype(HALF)


def prepare_kernel(
    place_ref,
    before_ref,
    dual_ref,
    base_ref,
    monitored_ref,
    ratings_ref,
    floor_ref,
    span_ref,
    limit_ref,
    on_ref,
    cost_ref,
    ramp_ref,
    dual_out,
    base_out,
    rating_out,
    unit_out,
    cost_out,
    ramp_out,
):
    ctgs, lines = monitored_ref.shape
    width = floor_ref.shape[1] // 2
    place = place_ref[0]
    table = ratings_ref[...].T
    hi = table.astype(HALF)
    left = table - hi.astype(FULL)
    mid = left.astype(HALF)
    lo = (left - mid.astype(FULL)).astype(HALF)
    groups = table.shape[1]
    for k in range(ctgs):
        cols = pl.ds(k * lines, lines)
        dual_out[:, cols] = dual_ref[:, k, :]
        base_out[:, cols] = base_ref[:, k, :]
        index = monitored_ref[k : k + 1, :]
        group = lax.broadcasted_iota(jnp.int32, (groups, lines), 0)
        chosen = (group == index // LANES).astype(FULL).astype(HALF)
        picked = (
            jnp.dot(hi, chosen, preferred_element_type=FULL)
            + jnp.dot(mid, chosen, preferred_element_type=FULL)
            + jnp.dot(lo, chosen, preferred_element_type=FULL)
        )
        lane = lax.broadcasted_iota(jnp.int32, (LANES, lines), 0)
        rating_out[:, cols] = jnp.sum(jnp.where(lane == index % LANES, picked, 0.0), axis=0, keepdims=True)
    for s in range(2):
        cols, own = pl.ds(s * width, width), pl.ds(own_first(place, s, width), width)
        floor = floor_ref[:, own]
        unit_out[0:1, cols] = floor
        unit_out[1:2, cols] = floor + span_ref[:, own]
        unit_out[2:3, cols] = limit_ref[:, own]
        unit_out[3:4, cols] = on_ref[:, own].astype(FULL)
        cost_out[:, cols] = cost_ref[:, own]
        ramp_out[:, cols] = ramp_ref[:, own]


def turn_kernel(first_ctg, masked_ref, before_ref, out_ref):
    ctgs, units, lines = out_ref.shape
    for k in range(ctgs):
        for at in range(0, units, WIDE):
            out_ref[k, pl.ds(at, WIDE), :] = masked_ref[first_ctg + k, :, pl.ds(at, WIDE)].T


def starting_levels(piece, devices, place, message_ref, all_hours, quarter):
    hours = all_hours // devices
    levels = message_ref[all_hours:, :quarter]
    shape = (all_hours, levels.shape[0])
    hour = lax.broadcasted_iota(jnp.int32, shape, 0)
    row = lax.broadcasted_iota(jnp.int32, shape, 1)
    apart = place ^ (hour // hours) ^ (piece % 2)
    block = parity(apart)
    for bit, mask in enumerate(mask_order(devices, piece // 2, True)):
        block = block + ((apart // mask) % 2) * 2 ** (bit + 1)
    chosen = (row // (2 * hours) == block) & (row % hours == hour % hours)
    return jnp.dot(chosen.astype(FULL).astype(HALF), levels, preferred_element_type=FULL)


def primal_piece(piece, step_size, stat_ref, message_ref, levels, unit_ref, moved_ref):
    all_hours, quarter = levels.shape
    cols = pl.ds(piece_at(piece, unit_ref.shape[1]), quarter)
    primal_step = step_size / stat_ref[0:1, 0:1]
    gradient = message_ref[:all_hours, :quarter].astype(FULL)
    moved = jnp.clip(levels - primal_step * gradient, unit_ref[0:1, cols], unit_ref[1:2, cols])
    moved_ref[...] = moved
    return (2.0 * moved - levels).astype(HALF)


def piece_flows(piece, half, turned_refs, k):
    turned_ref = turned_refs[k // turned_refs[0].shape[0]]
    rows = pl.ds(piece_at(piece, turned_ref.shape[1]), half.shape[1])
    return jnp.dot(half, turned_ref[k % turned_refs[0].shape[0], rows, :], preferred_element_type=FULL)


def flow_kernel(step_size, pieces, devices, turns, first, *refs):
    refs = list(refs)
    turned_refs = [refs.pop(0) for _ in range(turns)]
    place_ref, unit_ref = refs[:2]
    del refs[:2]
    leading = pieces[0] == 0
    stat_ref = None if first and leading else refs.pop(0)
    flow_ref = None if leading else refs.pop(0)
    message_refs = [refs.pop(0) for _ in pieces]
    level_refs = [refs.pop(0) for _ in pieces]
    moved_refs = [refs.pop(0) for _ in pieces]
    flow_out = refs.pop(0)
    all_hours, quarter = moved_refs[0].shape
    if leading:
        stat_out = refs.pop(0)
        if first:
            stat_out[...] = jnp.full(stat_out.shape, 1.0, FULL)
        else:
            dual_sq = total(message_refs[0][:SUMMANDS, quarter:].astype(FULL))
            primal_sq = stat_ref[1:2, 0:1]
            ratio = (dual_sq + 1e-06) / (primal_sq + 1e-06)
            weight = jnp.sqrt(stat_ref[0:1, 0:1]) * jnp.sqrt(jnp.sqrt(ratio))
            stat_out[...] = jnp.broadcast_to(weight, stat_out.shape)
        stat_ref = stat_out
    halves = []
    for piece, message_ref, level_ref, moved_ref in zip(pieces, message_refs, level_refs, moved_refs):
        if first:
            level_ref[...] = starting_levels(piece, devices, place_ref[0], message_ref, all_hours, quarter)
        halves.append(primal_piece(piece, step_size, stat_ref, message_ref, level_ref[...], unit_ref, moved_ref))
    lines = turned_refs[0].shape[2]
    for k in range(turns * turned_refs[0].shape[0]):
        at = pl.ds(k * lines, lines)
        part = None if flow_ref is None else flow_ref[:, at]
        for piece, half in zip(pieces, halves):
            flows = piece_flows(piece, half, turned_refs, k)
            part = flows if part is None else part + flows
        flow_out[:, at] = part


def dual_kernel(step_size, balance, devices, turns, first, last, *refs):
    refs = list(refs)
    turned_refs = [refs.pop(0) for _ in range(turns)]
    place_ref, masked_ref, message_ref = refs[:3]
    del refs[:3]
    level_refs = [refs.pop(0) for _ in range(3 if first else 4)]
    moved_refs = [refs.pop(0) for _ in range(3)]
    stat_ref, flow_ref, dual_ref, base_ref, rating_ref, unit_ref, cost_ref, demand_ref, ramp_ref = refs[:9]
    del refs[:9]
    price_ref = None if first else refs.pop(0)
    if first:
        level_refs.append(refs.pop())
    if last:
        level_out, dual_out, ramp_out, price_out, last_moved = refs
    else:
        last_moved, dual_out, ramp_out, price_out, stat_out, send_ref, half_dual, term_out = refs
    moved_refs = moved_refs + [last_moved]

    ctgs, lines, units = masked_ref.shape
    width, quarter = units // 2, units // 4
    all_hours, hours = level_refs[0].shape[0], cost_ref.shape[0]
    place = place_ref[0]
    first_hour = place * hours
    weight = stat_ref[0:1, 0:1]
    dual_step = step_size * weight

    if first:
        level_refs[3][...] = starting_levels(3, devices, place, message_ref, all_hours, quarter)
    half = primal_piece(3, step_size, stat_ref, message_ref, level_refs[3][...], unit_ref, last_moved)
    flow_acc = jnp.zeros((all_hours, lines), FULL)
    for k in range(ctgs):
        at = pl.ds(k * lines, lines)
        flows = flow_ref[:, at] + piece_flows(3, half, turned_refs, k)
        old = dual_ref[:, at]
        trial = old + dual_step * flows
        base, rating = base_ref[:, at], rating_ref[:, at]
        new = trial - jnp.clip(trial, dual_step * (base - rating), dual_step * (base + rating))
        if last:
            dual_out[:, k, :] = new
        else:
            dual_out[:, at] = new
            half_dual[:, at] = new.astype(HALF)
            flow_acc = flow_acc + (new - old) ** 2

    places = [pl.ds(piece_at(piece, units), quarter) for piece in range(PIECES)]
    moved_sq = None if last else total(flow_acc)
    supply = [jnp.zeros((1, 1), FULL) for _ in range(hours)]
    ramps = [[] for _ in range(hours)]
    for piece in range(PIECES):
        at = places[piece]
        ramp_limit, ramp_on = unit_ref[2:3, at], unit_ref[3:4, at]
        rows = []
        for j in range(hours + 1):
            spot = pl.ds(jnp.minimum(first_hour + j, all_hours - 1), 1)
            rows.append(2.0 * moved_refs[piece][spot, :] - level_refs[piece][spot, :])
        for j in range(hours):
            old = ramp_ref[j : j + 1, at]
            trial = old + dual_step * (ramp_on * (rows[j + 1] - rows[j]))
            reach = dual_step * ramp_limit
            new = trial - jnp.clip(trial, -reach, reach)
            supply[j] = supply[j] + jnp.sum(rows[j], axis=1, keepdims=True)
            ramps[j].append(new)
            if last:
                own = pl.multiple_of(own_first(place, piece % 2, width) + (piece // 2) * quarter, LANES)
                level_out[j : j + 1, pl.ds(own, quarter)] = moved_refs[piece][pl.ds(first_hour + j, 1), :]
                ramp_out[j : j + 1, pl.ds(own, quarter)] = new
            else:
                ramp_out[j : j + 1, at] = new
                moved_sq = moved_sq + total((new - old) ** 2)
    prices = []
    for j in range(hours):
        old = jnp.zeros((1, 1), FULL) if first else price_ref[j : j + 1, :]
        new = old + dual_step * (balance * (supply[j] - demand_ref[0:1, j : j + 1]))
        prices.append(balance * new)
        if last:
            price_out[j] = new[0, 0]
        else:
            price_out[j : j + 1, :] = new
            moved_sq = moved_sq + (new - old) ** 2
    if last:
        return

    primal_acc = jnp.zeros((all_hours, quarter), FULL)
    for piece in range(PIECES):
        primal_acc = primal_acc + (moved_refs[piece][...] - level_refs[piece][...]) ** 2
    row = lax.broadcasted_iota(jnp.int32, stat_out.shape, 0)
    stat_out[...] = jnp.where(row == 0, weight, total(primal_acc))
    for piece in range(PIECES):
        at = places[piece]
        terms = hour_terms(
            [cost_ref[j : j + 1, at] for j in range(hours)],
            [ramps[j][piece] for j in range(hours)],
            unit_ref[3:4, at],
            prices,
        )
        for j, term in enumerate(terms):
            term_out[j : j + 1, at] = term
    block = scalar_block(moved_sq, place, (all_hours, LANES))
    pull_piece(1, hours, first_hour, masked_ref, half_dual, term_out, send_ref)
    send_ref[:, quarter:] = block


def pull_piece(piece, hours, first_hour, masked_ref, half_dual, term_ref, out_ref):
    ctgs, lines, units = masked_ref.shape
    whole = masked_ref.reshape(ctgs * lines, units)
    for at in range(0, units // 4, WIDE):
        cols = pl.ds(piece_at(piece, units) + at, WIDE)
        pulled = jnp.dot(half_dual[...], whole[:, cols], preferred_element_type=FULL)
        terms = [term_ref[j : j + 1, cols] for j in range(hours + 1)]
        out_ref[:, pl.ds(at, WIDE)] = add_rows(pulled, first_hour, terms).astype(HALF)


def middle_pull_kernel(hours, place_ref, masked_ref, half_dual, term_ref, send_a, keep_a, send_b):
    quarter = send_b.shape[1]
    pull_piece(0, hours, place_ref[0] * hours, masked_ref, half_dual, term_ref, keep_a)
    keep_a[:, quarter:] = send_a[:, quarter:]
    pull_piece(3, hours, place_ref[0] * hours, masked_ref, half_dual, term_ref, send_b)


def last_pull_kernel(hours, place_ref, masked_ref, half_dual, term_ref, keep_b):
    pull_piece(2, hours, place_ref[0] * hours, masked_ref, half_dual, term_ref, keep_b)


def add_kernel(own_ref, received_ref, before_ref, out_ref):
    out_ref[...] = (own_ref[...].astype(FULL) + received_ref[...].astype(FULL)).astype(HALF)


def add_after(own, received, before):
    return call(add_kernel, "add", 0.1, [own, received, before], [near(*own.shape, dtype=HALF)])[0]


def join_kernel(all_hours, own_ref, received_ref, *refs):
    out_ref, scratch_ref = refs[-2:]
    extra = own_ref.shape[0] - all_hours
    own, received = own_ref[...].astype(FULL), received_ref[...].astype(FULL)
    scratch_ref[:all_hours, :] = own[:all_hours] + received[:all_hours]
    scratch_ref[all_hours : all_hours + extra, :] = own[all_hours:]
    scratch_ref[all_hours + extra :, :] = received[all_hours:]
    if out_ref is not None:
        out_ref[...] = scratch_ref[...].astype(HALF)


def split_kernel(all_hours, own_ref, received_ref, a_ref, b_ref, scratch_ref):
    join_kernel(all_hours, own_ref, received_ref, None, scratch_ref)
    quarter = b_ref.shape[1]
    a_ref[...] = scratch_ref[:, :quarter].astype(HALF)
    b_ref[...] = scratch_ref[:, quarter:].astype(HALF)


def first_join(all_hours, own, received):
    rows, quarter = 2 * own.shape[0] - all_hours, own.shape[1] // 2
    return call(
        functools.partial(split_kernel, all_hours),
        "split",
        0.3,
        [own, received],
        [near(rows, quarter, dtype=HALF)] * 2,
        [near(rows, 2 * quarter)],
    )


def join(all_hours, own, received, *before):
    shape = (2 * own.shape[0] - all_hours, own.shape[1])
    kernel = functools.partial(join_kernel, all_hours)
    return call(kernel, "join", 0.2, [own, received, *before], [near(*shape, dtype=HALF)], [near(*shape)])[0]


def exchange(x, mask):
    devices = lax.axis_size("ctg")
    flip = 0 if mask == 1 else 1
    return lax.ppermute(x, "ctg", [(i, i ^ mask ^ flip) for i in range(devices)])


def mask_order(devices, q, first):
    masks = [1 << b for b in range(1, devices.bit_length() - 1)]
    turn, back = ORDERS[(2 if first else 0) + q]
    masks = masks[turn:] + masks[:turn]
    return masks[::-1] if back else masks


def body(
    flow_tiles,
    tile_pattern,
    monitored,
    ratings,
    base_flow,
    unit_cost,
    unit_floor,
    unit_span,
    ramp_limit,
    ramp_mask,
    demand,
    start_output,
    start_flow_dual,
    start_ramp_dual,
):
    ctgs, lines, units = flow_tiles.shape
    all_hours, hours = start_flow_dual.shape[0], start_output.shape[0]
    devices = lax.axis_size("ctg")
    here = lax.axis_index("ctg").astype(jnp.int32).reshape(1)
    quarter = units // 4
    assert devices & (devices - 1) == 0 and 2 <= devices <= LANES and quarter % WIDE == 0
    step_size = 0.5 / (2.0 + math.sqrt(ctgs * devices * lines / units))
    balance = 1.0 / math.sqrt(units)
    spread = -ratings.shape[0] % (8 * LANES)
    table = jnp.pad(ratings, (0, spread)).reshape(-1, LANES)
    row = lambda x: x.reshape(1, units)
    start_rows = all_hours + 2 * hours
    start = near(start_rows, 2 * quarter, dtype=HALF)
    message_a, message_b = near(all_hours, quarter + LANES, dtype=HALF), near(all_hours, quarter, dtype=HALF)

    operands = [flow_tiles, start_flow_dual, row(ramp_mask), unit_cost, start_ramp_dual, start_output]
    masked, send, keep = pl.pallas_call(
        start_kernel,
        out_shape=(near(ctgs, lines, units, dtype=HALF), start, start),
        in_specs=[SMEM, HBM, HBM] + [VMEM] * 5,
        out_specs=(VMEM,) * 3,
        scratch_shapes=[
            pltpu.SMEM(tile_pattern.shape, jnp.int32),
            near(all_hours, units),
            pltpu.SemaphoreType.DMA((ctgs, 2)),
            pltpu.SemaphoreType.DMA,
        ],
        compiler_params=pltpu.CompilerParams(vmem_limit_bytes=46 * MIB),
        name="start",
    )(here, far(tile_pattern), *[far(x) for x in operands])
    masked = pltpu.with_memory_space_constraint(masked, pltpu.VMEM)
    demands = demand.reshape(1, hours)
    price, stat, levels, turned = None, None, None, []
    for iteration in range(ITERS):
        first, last = iteration == 0, iteration == ITERS - 1
        merge = functools.partial(join, all_hours) if first else jnp.add
        if first:
            owns = list(first_join(all_hours, keep, exchange(send, 1)))
        else:
            owns = [keep_a + exchange(send_a, 1), keep_b + exchange(send_b, 1)]
        orders = [mask_order(devices, q, first) for q in range(2)]
        steps = len(orders[0])
        for step in range(steps):
            before = []
            if first and step == steps - 2:
                operands = [start_flow_dual, base_flow, monitored, table, row(unit_floor), row(unit_span)]
                operands += [row(ramp_limit), row(ramp_mask), unit_cost, start_ramp_dual]
                dual, base, rating, unit, cost, ramp = call(
                    prepare_kernel,
                    "prepare",
                    1.5,
                    [here, owns[0], *[far(x) for x in operands]],
                    [
                        near(all_hours, ctgs * lines),
                        near(all_hours, ctgs * lines),
                        near(1, ctgs * lines),
                        near(4, units),
                        near(hours, units),
                        near(hours, units),
                    ],
                    smem=(0,),
                )
                before.append(rating)
            if first:
                share = [0] * (steps - len(TURNS)) + [ctgs * part // 8 for part in TURNS]
                for turn in range(sum(share[:step]), sum(share[: step + 1])):
                    turned += call(
                        functools.partial(turn_kernel, turn),
                        "turn",
                        0.45,
                        [masked, owns[0]],
                        [near(1, units, lines, dtype=HALF)],
                    )
                before += turned
            owns[0] = merge(owns[0], exchange(owns[0], orders[0][step]), *before)
            if first or step < steps - 1:
                owns[1] = merge(owns[1], exchange(owns[1], orders[1][step]))
        messages = [owns[0], exchange(owns[0], 1)]
        moved, flows = [], None
        levels = [] if first else levels
        for pieces in ((0,), (1, 2)):
            if 2 in pieces:
                if not first:
                    owns[1] = add_after(owns[1], exchange(owns[1], orders[1][-1]), stat)
                messages += [owns[1], exchange(owns[1], 1)]
            operands = [*turned, here, unit]
            operands += [] if first and flows is None else [stat]
            operands += [] if flows is None else [flows]
            operands += [messages[piece] for piece in pieces]
            operands += [] if first else [levels[piece] for piece in pieces]
            out_shape = [near(all_hours, quarter)] * (len(pieces) * (2 if first else 1))
            out_shape += [near(all_hours, ctgs * lines)]
            out_shape += [near(8, LANES)] if flows is None else []
            kernel = functools.partial(flow_kernel, step_size, pieces, devices, len(turned), first)
            outs = call(kernel, "flow", 0.7 * len(pieces), operands, out_shape, smem=(len(turned),))
            if flows is None:
                stat = outs.pop()
            flows = outs.pop()
            if first:
                levels += outs[: len(pieces)]
            moved += outs[-len(pieces) :]
        operands = [*turned, here, masked, messages[3], *levels, *moved, stat, flows, dual, base, rating, unit, cost]
        operands += [demands, ramp] if first else [demands, ramp, price]
        kernel = functools.partial(dual_kernel, step_size, balance, devices, len(turned), first, last)
        smem = (len(turned),)
        if last:
            f32 = lambda *shape: jax.ShapeDtypeStruct(shape, FULL)
            out_shape = [f32(hours, units), f32(all_hours, ctgs, lines), f32(hours, units), f32(hours)]
            return tuple(call(kernel, "dual", 1.2, operands, out_shape, [near(all_hours, quarter)], smem, (3,)))
        out_shape = [near(all_hours, quarter), near(all_hours, ctgs * lines), near(hours, units), near(hours, 1)]
        out_shape += [near(8, LANES), message_a, near(all_hours, ctgs * lines, dtype=HALF), near(8, units)]
        scratch = [near(all_hours, quarter)] if first else []
        outs = call(kernel, "dual", 1.5, operands, out_shape, scratch, smem)
        levels = (*moved, outs[0])
        dual, ramp, price, stat, send_a, half_dual, terms = outs[1:]
        operands = [here, masked, half_dual, terms]
        keep_a, send_b = call(
            functools.partial(middle_pull_kernel, hours),
            "pull",
            1.2,
            [*operands, send_a],
            [message_a, message_b],
            smem=(0,),
        )
        (keep_b,) = call(functools.partial(last_pull_kernel, hours), "pull", 0.6, operands, [message_b], smem=(0,))


def solution(mesh):
    return jax.shard_map(
        body,
        mesh=mesh,
        in_specs=(
            P("ctg", None, None),
            P("ctg", None, None),
            P("ctg", None),
            P(),
            P("grp", "ctg", None),
            P(("grp", "ctg"), None),
            P(),
            P(),
            P(),
            P(),
            P(("grp", "ctg")),
            P(("grp", "ctg"), None),
            P("grp", "ctg", None),
            P(("grp", "ctg"), None),
        ),
        out_specs=(
            P(("grp", "ctg"), None),
            P("grp", "ctg", None),
            P(("grp", "ctg"), None),
            P(("grp", "ctg")),
        ),
        check_vma=False,
    )
```
